256 devices in a mesh: grp: 4 (over z_hi), dev: 64 (over y, z_lo, x, core).
Axes of the slice: x: 4, y: 4, z: 8 (z_hi: 4, z_lo: 2; z = z_hi * 2 + z_lo), core: 2. Of those that a mesh axis runs over, the one named last changes fastest.
Arguments:
- adjoint: float32 [16, 8, 512, 8, 128], P('grp', None, 'dev'), may hold values from -6 to 6
- right_side: float32 [16, 8, 512, 8, 128], P('grp', None, 'dev'), may hold values from -6 to 6
- velocity: float32 [3, 16, 8, 512, 8, 128], P(None, 'grp', None, 'dev'), may hold values from -1.2 to 1.2
- conductivity: float32 [16, 8, 512, 8, 128], P('grp', None, 'dev'), may hold values from 0.002 to 0.02
- mass_term: float32 [16, 8, 512, 8, 128], P('grp', None, 'dev'), may hold values from 0.5 to 2
- fdm_inverse: float32 [16, 8, 512, 8, 128], P('grp', None, 'dev'), may hold values from 0.05 to 1
- coarse_factor: float32 [8192, 8192], P(('grp', 'dev')), may hold values from -0.5 to 0.5
Outputs:
- residual: float32 [16, 8, 512, 8, 128], P('grp', None, 'dev')
- correction: float32 [16, 8, 512, 8, 128], P('grp', None, 'dev')
The draws below stay inside these ranges and needn't reach their ends.
All inputs are finite; a program needn't handle non-finite values.
Results may differ from the reference program's by a relative error of at most 0.0003.
Values sent between devices are 32-bit elements; how exact they have to be, the bound alone decides.
A program may use at most 64 MiB of HBM per device.

```python
import math
import jax
import jax.numpy as jnp
from jax import lax

NODES = 8
EXD = 4
EYD = 8
NZ = 128
GX = 16
GY = 512
NC = 8192
N_GRP = 4
N_DEV = 64


def levels(own_key, extent, shards, least, high):
    level, own = 1.0, jax.random.fold_in(own_key, 6)
    for dim, blocks in shards:
        heights = jnp.exp(jax.random.uniform(jax.random.fold_in(own, dim), (blocks,), jnp.float32, least / len(shards), high / len(shards)))
        level = level * jnp.repeat(heights, extent[dim] // blocks).reshape([-1 if axis == dim else 1 for axis in range(len(extent))])
    return level


def bell_draw(stream_key, shape, deviation, reach, shards=(), dtype=jnp.bfloat16):
    entries = deviation * jax.random.normal(stream_key, shape, jnp.float32)
    if shards:
        entries = entries * levels(stream_key, shape, shards, -0.22, 0.18)
    return jnp.clip(entries, -reach, reach).astype(dtype)


def setup_inputs(seed: int = 0) -> dict:
    key_of = jax.random.split(jax.random.key(seed), 8)
    adjoint = bell_draw(key_of[0], (GX, NODES, GY, NODES, NZ), 1.0, 6.0, ((0, 4), (2, 64)), jnp.float32)
    right_side = bell_draw(key_of[1], (GX, NODES, GY, NODES, NZ), 1.0, 6.0, ((0, 4), (2, 64)), jnp.float32)
    velocity = bell_draw(key_of[2], (3, GX, NODES, GY, NODES, NZ), 0.2, 1.2, ((1, 4), (3, 64)), jnp.float32)
    conductivity = jnp.clip(jnp.exp(math.log(0.02) - 2.30258502 * jax.random.uniform(key_of[3], (GX, NODES, GY, NODES, NZ), jnp.float32) ** levels(key_of[3], (GX, NODES, GY, NODES, NZ), ((0, 4), (2, 64)), -0.2, 0.2)), 0.002, 0.02)
    mass_term = jnp.clip(jnp.exp(math.log(2.0) - 1.3862944 * jax.random.uniform(key_of[4], (GX, NODES, GY, NODES, NZ), jnp.float32) ** levels(key_of[4], (GX, NODES, GY, NODES, NZ), ((0, 4), (2, 64)), -0.2, 0.2)), 0.5, 2.0)
    fdm_inverse = jnp.clip(jnp.exp(math.log(1.0) - 2.9957323 * jax.random.uniform(key_of[5], (GX, NODES, GY, NODES, NZ), jnp.float32) ** levels(key_of[5], (GX, NODES, GY, NODES, NZ), ((0, 4), (2, 64)), -0.2, 0.2)), 0.05, 1.0)
    coarse_factor = bell_draw(key_of[6], (NC, NC), (NC // 64) ** -0.5, 0.5, ((0, 256),), jnp.float32)
    return dict(adjoint=adjoint, right_side=right_side, velocity=velocity, conductivity=conductivity, mass_term=mass_term, fdm_inverse=fdm_inverse, coarse_factor=coarse_factor)


GLL_POINTS = [-1.0, -0.871740148509607, -0.591700181433142, -0.209299217902479, 0.209299217902479, 0.591700181433142, 0.871740148509607, 1.0]
HIGHEST_PRECISION = lax.Precision.HIGHEST


def legendre_value(point, highest):
    previous = 1.0
    current = point
    for degree in range(1, highest):
        previous, current = current, ((2 * degree + 1) * point * current - degree * previous) / (degree + 1)
    return current


def identity_list(dimension):
    return [[1.0 if row_index == col_index else 0.0 for col_index in range(dimension)] for row_index in range(dimension)]


def transpose_list(matrix):
    return [[matrix[row_index][col_index] for row_index in range(len(matrix))] for col_index in range(len(matrix[0]))]


def matrix_product(left, right):
    inner_size = len(right)
    return [[sum(left[row_index][inner] * right[inner][col_index] for inner in range(inner_size)) for col_index in range(len(right[0]))] for row_index in range(len(left))]


def jacobi_eigen(matrix):
    current = [list(line) for line in matrix]
    dimension = len(matrix)
    rotations = identity_list(dimension)
    for repeat in range(12):
        for row_index in range(dimension - 1):
            for col_index in range(row_index + 1, dimension):
                angle = 0.5 * math.atan2(2.0 * current[row_index][col_index], current[row_index][row_index] - current[col_index][col_index])
                cosine = math.cos(angle)
                sine_value = math.sin(angle)
                rotation = identity_list(dimension)
                rotation[row_index][row_index] = cosine
                rotation[col_index][col_index] = cosine
                rotation[row_index][col_index] = -sine_value
                rotation[col_index][row_index] = sine_value
                current = matrix_product(matrix_product(transpose_list(rotation), current), rotation)
                rotations = matrix_product(rotations, rotation)
    ordering = sorted(range(dimension), key=lambda position: current[position][position])
    return [[rotations[row_index][position] for position in ordering] for row_index in range(dimension)]


def element_tables():
    total_points = len(GLL_POINTS)
    weights_bary = []
    for row_index in range(total_points):
        product_value = 1.0
        for col_index in range(total_points):
            if col_index != row_index:
                product_value = product_value * (GLL_POINTS[row_index] - GLL_POINTS[col_index])
        weights_bary.append(1.0 / product_value)
    derivative = [[0.0] * total_points for row_index in range(total_points)]
    for row_index in range(total_points):
        for col_index in range(total_points):
            if col_index != row_index:
                derivative[row_index][col_index] = (weights_bary[col_index] / weights_bary[row_index]) / (GLL_POINTS[row_index] - GLL_POINTS[col_index])
        derivative[row_index][row_index] = -sum(derivative[row_index])
    quadrature = [2.0 / ((total_points - 1) * total_points * legendre_value(point, total_points - 1) ** 2) for point in GLL_POINTS]
    stiffness = [[sum(derivative[inner][row_index] * quadrature[inner] * derivative[inner][col_index] for inner in range(total_points)) + (quadrature[row_index] if row_index == col_index else 0.0) for col_index in range(total_points)] for row_index in range(total_points)]
    return derivative, jacobi_eigen(stiffness)


def block_diagonal(blocks, matrix):
    node_count = len(matrix)
    total = blocks * node_count
    return [[matrix[row_index % node_count][col_index % node_count] if row_index // node_count == col_index // node_count else 0.0 for col_index in range(total)] for row_index in range(total)]


def assembly_table(blocks, node_count):
    total = blocks * node_count
    shared_index = [(position // node_count) * (node_count - 1) + position % node_count for position in range(total)]
    return [[1.0 if shared_index[row_index] == shared_index[col_index] else 0.0 for col_index in range(total)] for row_index in range(total)]


def along_first(matrix, field):
    return jnp.einsum("ai,xiyjz->xayjz", matrix, field, precision=HIGHEST_PRECISION)


def along_second(matrix, field):
    return jnp.einsum("bj,xiyjz->xiybz", matrix, field, precision=HIGHEST_PRECISION)


def along_third(field, table):
    return jnp.einsum("xiyjz,zw->xiyjw", field, table, precision=HIGHEST_PRECISION)


def to_grid(field, axis_elem):
    elements = field.shape[axis_elem]
    node_count = field.shape[axis_elem + 1]
    lower_face = lax.index_in_dim(field, 0, axis_elem + 1, keepdims=False)
    upper_face = lax.index_in_dim(field, node_count - 1, axis_elem + 1, keepdims=False)
    interior = lax.slice_in_dim(field, 1, node_count - 1, axis=axis_elem + 1)
    joints = jnp.concatenate([lax.slice_in_dim(lower_face, 0, 1, axis=axis_elem), lax.slice_in_dim(upper_face, 0, elements - 1, axis=axis_elem) + lax.slice_in_dim(lower_face, 1, elements, axis=axis_elem), lax.slice_in_dim(upper_face, elements - 1, elements, axis=axis_elem)], axis=axis_elem)
    leading = jnp.concatenate([jnp.expand_dims(lax.slice_in_dim(joints, 0, elements, axis=axis_elem), axis_elem + 1), interior], axis=axis_elem + 1)
    new_shape = leading.shape[:axis_elem] + (elements * (node_count - 1),) + leading.shape[axis_elem + 2:]
    merged = leading.reshape(new_shape)
    return jnp.concatenate([merged, lax.slice_in_dim(joints, elements, elements + 1, axis=axis_elem)], axis=axis_elem)


def from_grid(grid, axis_elem, elements, node_count):
    span = elements * (node_count - 1)
    leading = lax.slice_in_dim(grid, 0, span, axis=axis_elem)
    split_shape = leading.shape[:axis_elem] + (elements, node_count - 1) + leading.shape[axis_elem + 1:]
    leading = leading.reshape(split_shape)
    trailing = lax.slice_in_dim(grid, node_count - 1, span + 1, stride=node_count - 1, axis=axis_elem)
    return jnp.concatenate([leading, jnp.expand_dims(trailing, axis_elem + 1)], axis=axis_elem + 1)


def assemble(field, z_table):
    field = along_third(field, z_table)
    elements_first = field.shape[0]
    elements_second = field.shape[2]
    node_count = field.shape[1]
    grid = to_grid(to_grid(field, 0), 1)
    return from_grid(from_grid(grid, 1, elements_second, node_count), 0, elements_first, node_count)


def reference(adjoint, right_side, velocity, conductivity, mass_term, fdm_inverse, coarse_factor):
    derivative, eigen_vectors = element_tables()
    node_count = adjoint.shape[1]
    blocks = adjoint.shape[4] // node_count
    derivative_table = jnp.asarray(derivative, jnp.float32)
    vectors_table = jnp.asarray(eigen_vectors, jnp.float32)
    backward_list = block_diagonal(blocks, derivative)
    vectors_list = block_diagonal(blocks, eigen_vectors)
    forward_z = jnp.asarray(transpose_list(backward_list), jnp.float32)
    backward_z = jnp.asarray(backward_list, jnp.float32)
    spectral_z = jnp.asarray(vectors_list, jnp.float32)
    physical_z = jnp.asarray(transpose_list(vectors_list), jnp.float32)
    z_table = jnp.asarray(assembly_table(blocks, node_count), jnp.float32)
    flux_first = conductivity * along_first(derivative_table, adjoint) + velocity[0] * adjoint
    flux_second = conductivity * along_second(derivative_table, adjoint) + velocity[1] * adjoint
    flux_third = conductivity * along_third(adjoint, forward_z) + velocity[2] * adjoint
    local = mass_term * adjoint + along_first(derivative_table.T, flux_first) + along_second(derivative_table.T, flux_second) + along_third(flux_third, backward_z)
    residual = right_side - assemble(local, z_table)
    column_means = jnp.sum(residual, axis=(1, 3, 4)) / float(node_count * node_count * adjoint.shape[4])
    coarse_rhs = column_means.reshape(N_GRP, EXD, N_DEV, EYD).transpose(0, 2, 1, 3).reshape(-1)
    inner_vector = jnp.dot(coarse_rhs, coarse_factor, precision=HIGHEST_PRECISION)
    coarse_values = jnp.dot(coarse_factor, inner_vector, precision=HIGHEST_PRECISION)
    coarse_field = coarse_values.reshape(N_GRP, N_DEV, EXD, EYD).transpose(0, 2, 1, 3).reshape(GX, GY)
    spectral = along_third(along_second(vectors_table.T, along_first(vectors_table.T, residual)), spectral_z)
    spectral = fdm_inverse * spectral
    local_solve = along_third(along_second(vectors_table, along_first(vectors_table, spectral)), physical_z)
    combined = local_solve + coarse_field[:, None, :, None, None]
    correction = assemble(combined, z_table)
    return residual, correction
```

```python
import functools
import math

import jax
import jax.numpy as jnp
import ml_dtypes
import numpy as np
from jax import lax
from jax.experimental import pallas as pl
from jax.experimental.pallas import tpu as pltpu
from jax.sharding import PartitionSpec as P

GLL_POINTS = [
    -1.0,
    -0.871740148509607,
    -0.591700181433142,
    -0.209299217902479,
    0.209299217902479,
    0.591700181433142,
    0.871740148509607,
    1.0,
]


def legendre_value(point, highest):
    previous = 1.0
    current = point
    for degree in range(1, highest):
        previous, current = (
            current,
            ((2 * degree + 1) * point * current - degree * previous) / (degree + 1),
        )
    return current


def identity_list(dimension):
    return [
        [1.0 if row_index == col_index else 0.0 for col_index in range(dimension)]
        for row_index in range(dimension)
    ]


def transpose_list(matrix):
    return [
        [matrix[row_index][col_index] for row_index in range(len(matrix))]
        for col_index in range(len(matrix[0]))
    ]


def matrix_product(left, right):
    inner_size = len(right)
    return [
        [
            sum((left[row_index][inner] * right[inner][col_index] for inner in range(inner_size)))
            for col_index in range(len(right[0]))
        ]
        for row_index in range(len(left))
    ]


def jacobi_eigen(matrix):
    current = [list(line) for line in matrix]
    dimension = len(matrix)
    rotations = identity_list(dimension)
    for repeat in range(12):
        for row_index in range(dimension - 1):
            for col_index in range(row_index + 1, dimension):
                angle = 0.5 * math.atan2(
                    2.0 * current[row_index][col_index],
                    current[row_index][row_index] - current[col_index][col_index],
                )
                cosine = math.cos(angle)
                sine_value = math.sin(angle)
                rotation = identity_list(dimension)
                rotation[row_index][row_index] = cosine
                rotation[col_index][col_index] = cosine
                rotation[row_index][col_index] = -sine_value
                rotation[col_index][row_index] = sine_value
                current = matrix_product(
                    matrix_product(transpose_list(rotation), current), rotation
                )
                rotations = matrix_product(rotations, rotation)
    ordering = sorted(range(dimension), key=lambda position: current[position][position])
    return [
        [rotations[row_index][position] for position in ordering] for row_index in range(dimension)
    ]


def element_tables():
    total_points = len(GLL_POINTS)
    weights_bary = []
    for row_index in range(total_points):
        product_value = 1.0
        for col_index in range(total_points):
            if col_index != row_index:
                product_value = product_value * (GLL_POINTS[row_index] - GLL_POINTS[col_index])
        weights_bary.append(1.0 / product_value)
    derivative = [[0.0] * total_points for row_index in range(total_points)]
    for row_index in range(total_points):
        for col_index in range(total_points):
            if col_index != row_index:
                derivative[row_index][col_index] = (
                    weights_bary[col_index]
                    / weights_bary[row_index]
                    / (GLL_POINTS[row_index] - GLL_POINTS[col_index])
                )
        derivative[row_index][row_index] = -sum(derivative[row_index])
    quadrature = [
        2.0 / ((total_points - 1) * total_points * legendre_value(point, total_points - 1) ** 2)
        for point in GLL_POINTS
    ]
    stiffness = [
        [
            sum(
                (
                    derivative[inner][row_index] * quadrature[inner] * derivative[inner][col_index]
                    for inner in range(total_points)
                )
            )
            + (quadrature[row_index] if row_index == col_index else 0.0)
            for col_index in range(total_points)
        ]
        for row_index in range(total_points)
    ]
    return (derivative, jacobi_eigen(stiffness))


def block_diagonal(blocks, matrix):
    node_count = len(matrix)
    total = blocks * node_count
    return [
        [
            (
                matrix[row_index % node_count][col_index % node_count]
                if row_index // node_count == col_index // node_count
                else 0.0
            )
            for col_index in range(total)
        ]
        for row_index in range(total)
    ]


def assembly_table(blocks, node_count):
    total = blocks * node_count
    shared_index = [
        position // node_count * (node_count - 1) + position % node_count
        for position in range(total)
    ]
    return [
        [
            1.0 if shared_index[row_index] == shared_index[col_index] else 0.0
            for col_index in range(total)
        ]
        for row_index in range(total)
    ]

MESH_IDS = pl.DeviceIdType.MESH
TILE = 128
PACK = 16


def split_halves(values):
    high = values.astype(jnp.bfloat16)
    return high, (values - high.astype(jnp.float32)).astype(jnp.bfloat16)


def lane_operator(table, field):
    high, low = split_halves(field)
    stacked = jnp.concatenate([table, table], axis=0)
    product = jnp.dot(
        jnp.concatenate([high, low], axis=1), stacked, preferred_element_type=jnp.float32
    )
    return product[:, :TILE] + product[:, TILE:]


def row_operator(table, field):
    high, low = split_halves(field)
    stacked = jnp.concatenate([table, table], axis=1)
    results = []
    for start in range(0, field.shape[0], 2 * TILE):
        first, second = slice(start, start + TILE), slice(start + TILE, start + 2 * TILE)
        operand = jnp.concatenate(
            [
                jnp.concatenate([high[first], low[first]], axis=0),
                jnp.concatenate([high[second], low[second]], axis=0),
            ],
            axis=1,
        )
        product = jnp.dot(stacked, operand, preferred_element_type=jnp.float32)
        summed = product[:TILE] + product[TILE:]
        results += [summed[:, :TILE], summed[:, TILE:]]
    return jnp.concatenate(results, axis=0)


def weighted(coefficients, terms):
    total = terms[0] * coefficients[0]
    for coefficient, term in zip(coefficients[1:], terms[1:]):
        total = total + term * coefficient
    return total


def mirrored(layers):
    count = len(layers)
    half = count // 2
    sums = [layers[k] + layers[count - 1 - k] for k in range(half)]
    gaps = [layers[k] - layers[count - 1 - k] for k in range(half)]
    return sums, gaps


def odd_operator(matrix, layers):
    count = len(layers)
    half = count // 2
    sums, gaps = mirrored(layers)
    lower, upper = [], []
    for row in range(half):
        line = matrix[row]
        even = weighted([0.5 * (line[k] + line[count - 1 - k]) for k in range(half)], sums)
        odd = weighted([0.5 * (line[k] - line[count - 1 - k]) for k in range(half)], gaps)
        lower.append(odd + even)
        upper.append(odd - even)
    return lower + upper[::-1]


def to_modes(vectors, layers):
    count = len(layers)
    half = count // 2
    sums, gaps = mirrored(layers)
    return [
        weighted([vectors[k][mode] for k in range(half)], gaps if mode % 2 else sums)
        for mode in range(count)
    ]


def from_modes(vectors, modes):
    count = len(modes)
    half = count // 2
    lower, upper = [], []
    for row in range(half):
        even = weighted(vectors[row][0::2], modes[0::2])
        odd = weighted(vectors[row][1::2], modes[1::2])
        lower.append(even + odd)
        upper.append(even - odd)
    return lower + upper[::-1]


def half_pair(matrix):
    table = np.asarray(matrix, np.float64).astype(np.float32)
    high = table.astype(ml_dtypes.bfloat16)
    low = (table - high.astype(np.float32)).astype(ml_dtypes.bfloat16)
    return high, low


def lane_table(matrix):
    return np.concatenate(half_pair(matrix), axis=1)


def row_table(matrix):
    return np.concatenate(half_pair(matrix), axis=0)


def operator_tables(nodes, lanes):
    derivative, vectors = element_tables()
    blocks = lanes // nodes
    backward_z = block_diagonal(blocks, derivative)
    vectors_z = block_diagonal(blocks, vectors)
    joined = assembly_table(blocks, nodes)
    physical_joined = (np.asarray(transpose_list(vectors_z)) @ np.asarray(joined)).tolist()
    lane_tables = np.stack(
        [
            lane_table(transpose_list(backward_z)),
            lane_table(backward_z),
            lane_table(vectors_z),
            lane_table(physical_joined),
        ]
    )
    row_tables = np.stack(
        [
            row_table(backward_z),
            row_table(transpose_list(backward_z)),
            row_table(transpose_list(vectors_z)),
            row_table(vectors_z),
        ]
    )
    return derivative, vectors, lane_tables, row_tables


class Layout:
    def __init__(self, elements_x, nodes, elements_y, lanes, groups, devices, coarse):
        self.ex, self.n, self.ey, self.lanes = elements_x, nodes, elements_y, lanes
        self.groups, self.devices = groups, devices
        self.slab = elements_y * nodes
        self.chunk = nodes * self.slab
        self.rows = elements_x * self.chunk
        self.lines = elements_x * nodes
        self.columns = elements_x * elements_y
        self.pack = math.gcd(PACK, devices)
        self.far = groups * (devices // self.pack)
        self.coarse = coarse
        self.coarse_lines = coarse // lanes
        self.share = self.coarse_lines // self.pack


def step_kernel(
    lay, derivative, vectors,
    adjoint, right_side, velocity, conductivity, mass_term, fdm_inverse, factor, lane_t, row_t,
    residual, correction,
    v_adj, v_rs, v_vel, v_con, v_mass, v_fdm, v_fac, v_lane, v_row,
    local, side_send, side_recv, row_send, row_recv, edge_recv, halo_lines,
    column_sum, inner_part, near_src, near_in, far_in, full_in,
    own_coarse, ring_x, ring_y, ring_d, grid_rows, coarse_tile,
    load_sem, face_send, face_recv, ring_send, ring_recv, sum_send, sum_recv,
):
    ex, n, ey, lanes = lay.ex, lay.n, lay.ey, lay.lanes
    slab, chunk, lines, columns = lay.slab, lay.chunk, lay.lines, lay.columns
    group = lax.axis_index("grp")
    device = lax.axis_index("dev")
    near_id = lax.rem(device, lay.pack)
    block_id = device // lay.pack
    far_blocks = lay.devices // lay.pack
    far_id = group * far_blocks + block_id

    def near_device(index):
        return (group, block_id * lay.pack + index)

    def far_device(index):
        return (index // far_blocks, lax.rem(index, far_blocks) * lay.pack + near_id)

    def neighbour(step_g, step_d):
        return (
            lax.rem(group + step_g + lay.groups, lay.groups),
            lax.rem(device + step_d + lay.devices, lay.devices),
        )

    steps = [(g, d) for g in (-1, 0, 1) for d in (-1, 0, 1) if (g, d) != (0, 0)]

    barrier = pltpu.get_barrier_semaphore()
    for step in steps:
        pl.semaphore_signal(barrier, inc=1, device_id=neighbour(*step), device_id_type=MESH_IDS)
    for offset in range(1, lay.pack):
        target = near_device(lax.rem(near_id + offset, lay.pack))
        pl.semaphore_signal(barrier, inc=1, device_id=target, device_id_type=MESH_IDS)
    for offset in range(1, lay.far):
        target = far_device(lax.rem(far_id + offset, lay.far))
        pl.semaphore_signal(barrier, inc=1, device_id=target, device_id_type=MESH_IDS)

    def chunk_rows(x):
        return pl.ds(pl.multiple_of(x * chunk, chunk), chunk)

    def chunk_loads(x):
        rows = chunk_rows(x)
        return [
            pltpu.make_async_copy(adjoint.at[rows], v_adj.at[rows], load_sem.at[0, x]),
            pltpu.make_async_copy(conductivity.at[rows], v_con.at[rows], load_sem.at[1, x]),
            pltpu.make_async_copy(velocity.at[:, rows], v_vel.at[:, rows], load_sem.at[2, x]),
            pltpu.make_async_copy(mass_term.at[rows], v_mass.at[rows], load_sem.at[3, x]),
        ]

    table_loads = [
        pltpu.make_async_copy(lane_t, v_lane, load_sem.at[4, 0]),
        pltpu.make_async_copy(row_t, v_row, load_sem.at[4, 1]),
    ]
    late_loads = [
        pltpu.make_async_copy(right_side, v_rs, load_sem.at[4, 2]),
        pltpu.make_async_copy(factor, v_fac, load_sem.at[4, 3]),
        pltpu.make_async_copy(fdm_inverse, v_fdm, load_sem.at[5, 0]),
    ]
    for copy in table_loads:
        copy.start()
    for x in range(ex):
        for copy in chunk_loads(x):
            copy.start()
    for copy in late_loads:
        copy.start()
    for copy in table_loads:
        copy.wait()

    lane_index = lax.broadcasted_iota(jnp.int32, (1, lanes), 1)
    lane_node = lax.rem(lane_index, n)
    is_upper = lane_node == n - 1
    shared = jnp.where(
        (is_upper & (lane_index != lanes - 1)) | ((lane_node == 0) & (lane_index != 0)), 1.0, 0.0
    ).astype(jnp.float32)
    line_index = lax.broadcasted_iota(jnp.int32, (n, lanes), 0)
    first_line = line_index == 0
    last_line = line_index == n - 1

    def layers_of(field):
        return [field[k * slab : (k + 1) * slab] for k in range(n)]

    def local_chunk(x, carry):
        for copy in chunk_loads(x):
            copy.wait()
        rows = chunk_rows(x)
        field = v_adj[rows]
        diffusion = v_con[rows]
        third = diffusion * lane_operator(v_lane[0], field) + v_vel[2, rows] * field
        total = lane_operator(v_lane[1], third)
        second = diffusion * row_operator(v_row[0], field) + v_vel[1, rows] * field
        total = total + row_operator(v_row[1], second)
        gradient = jnp.concatenate(odd_operator(derivative, layers_of(field)), axis=0)
        first = diffusion * gradient + v_vel[0, rows] * field
        total = total + jnp.concatenate(
            odd_operator(transpose_list(derivative), layers_of(first)), axis=0
        )
        total = total + v_mass[rows] * field
        crossed = jnp.where(
            is_upper, pltpu.roll(total, lanes - 1, axis=1), pltpu.roll(total, 1, axis=1)
        )
        local[rows] = total + shared * crossed
        return carry

    lax.fori_loop(0, ex, local_chunk, 0)

    low_g = jnp.where(group > 0, 1.0, 0.0).astype(jnp.float32)
    high_g = jnp.where(group < lay.groups - 1, 1.0, 0.0).astype(jnp.float32)
    low_d = jnp.where(device > 0, 1.0, 0.0).astype(jnp.float32)
    high_d = jnp.where(device < lay.devices - 1, 1.0, 0.0).astype(jnp.float32)
    gates_g, gates_d = (low_g, high_g), (low_d, high_d)

    def face_copies(phase):
        copies = []
        for index, (g, d) in enumerate(steps):
            if d == 0:
                source, target = side_send.at[phase, (g + 1) // 2], side_recv.at[phase, (1 - g) // 2]
            elif g == 0:
                source, target = row_send.at[phase, (d + 1) // 2], row_recv.at[phase, (1 - d) // 2]
            else:
                x = 0 if g < 0 else ex - 1
                source = row_send.at[phase, (d + 1) // 2, x]
                target = edge_recv.at[phase, (1 - g) // 2, (1 - d) // 2]
            copies.append(
                pltpu.make_async_remote_copy(
                    src_ref=source,
                    dst_ref=target,
                    send_sem=face_send.at[phase, index],
                    recv_sem=face_recv.at[phase, index],
                    device_id=neighbour(g, d),
                    device_id_type=MESH_IDS,
                )
            )
        return copies

    def send_faces(field, phase):
        side_send[phase, 0] = field[pl.ds(0, slab)]
        side_send[phase, 1] = field[pl.ds(lay.rows - slab, slab)]
        for x in range(ex - 1):
            upper, lower = pl.ds((x + 1) * chunk - slab, slab), pl.ds((x + 1) * chunk, slab)
            both = field[upper] + field[lower]
            field[upper] = both
            field[lower] = both
        for x in range(ex):
            row_send[phase, 0, x] = field[pl.ds(x * chunk, n, stride=slab)]
            row_send[phase, 1, x] = field[pl.ds(x * chunk + slab - 1, n, stride=slab)]
        copies = face_copies(phase)
        for copy in copies:
            copy.start()
        return copies

    def join_faces(field, phase, copies):
        for copy in copies:
            copy.wait_recv()
        head, tail = pl.ds(0, slab), pl.ds(lay.rows - slab, slab)
        field[head] = field[head] + low_g * side_recv[phase, 0]
        field[tail] = field[tail] + high_g * side_recv[phase, 1]
        for d in range(2):
            low_edge = edge_recv[phase, 0, d, pl.ds(n - 1, n, stride=0)]
            high_edge = edge_recv[phase, 1, d, pl.ds(0, n, stride=0)]
            first = row_recv[phase, d, 0] + jnp.where(first_line, low_g * low_edge, 0.0)
            row_recv[phase, d, 0] = first
            last = row_recv[phase, d, ex - 1] + jnp.where(last_line, high_g * high_edge, 0.0)
            row_recv[phase, d, ex - 1] = last
            spot = 0 if d == 0 else n - 1
            for x in range(ex):
                halo_lines[pl.ds(x * slab + spot, n, stride=n)] = gates_d[d] * row_recv[phase, d, x]
        starts = pl.ds(0, lines * ey, stride=n)
        ends = pl.ds(n - 1, lines * ey, stride=n)
        lower = field[starts].reshape(lines, ey, lanes)
        upper = field[ends].reshape(lines, ey, lanes)
        outside = halo_lines[...].reshape(lines, ey, lanes)
        from_below = jnp.where(first_line, outside, pltpu.roll(upper, 1, axis=1))
        from_above = jnp.where(last_line, outside, pltpu.roll(lower, ey - 1, axis=1))
        field[starts] = (lower + from_below).reshape(lines * ey, lanes)
        field[ends] = (upper + from_above).reshape(lines * ey, lanes)

    pl.semaphore_wait(barrier, len(steps) + lay.pack - 1 + lay.far - 1)
    first_copies = send_faces(local, 0)
    for copy in late_loads:
        copy.wait()
    join_faces(local, 0, first_copies)

    for x in range(ex):
        rows = pl.ds(x * chunk, chunk)
        value = v_rs[rows] - local[rows]
        residual[rows] = value
        layers = layers_of(value)
        total = layers[0]
        for layer in layers[1:]:
            total = total + layer
        column_sum[pl.ds(x * slab, slab)] = total
    summed = column_sum[pl.ds(0, columns, stride=n)]
    for j in range(1, n):
        summed = summed + column_sum[pl.ds(j, columns, stride=n)]
    means = jnp.sum(summed, axis=1, keepdims=True) * (1.0 / float(n * n * lanes))
    means = jnp.broadcast_to(means, (columns, lanes))

    def inner_block(block, carry):
        for k in range(8):
            line = block * 8 + k
            piece = v_fac[:, pl.ds(pl.multiple_of(line * lanes, lanes), lanes)] * means
            total = piece[0:8]
            for start in range(8, columns, 8):
                total = total + piece[start : start + 8]
            inner_part[pl.ds(pl.multiple_of(line * 8, 8), 8)] = total
        return carry

    lax.fori_loop(0, lay.coarse_lines // 8, inner_block, 0)
    for index in range(lay.pack):
        base = index * lay.share * 8
        total = inner_part[pl.ds(base, lay.share, stride=8)]
        for k in range(1, 8):
            total = total + inner_part[pl.ds(base + k, lay.share, stride=8)]
        near_src[index] = total

    def exchange(stage, count, own, device_of, source_of, buffer):
        def send(offset, carry):
            index = lax.rem(own + offset, count)
            pltpu.make_async_remote_copy(
                src_ref=source_of(index),
                dst_ref=buffer.at[own],
                send_sem=sum_send.at[stage],
                recv_sem=sum_recv.at[stage],
                device_id=device_of(index),
                device_id_type=MESH_IDS,
            ).start()
            return carry

        for offset in range(1, count):
            send(offset, 0)

    def await_exchange(stage, count, buffer, sem):
        part = buffer.at[pl.ds(0, count - 1)]
        pltpu.make_async_copy(part, part, sem.at[stage]).wait()

    exchange(0, lay.pack, near_id, near_device, lambda index: near_src.at[index], near_in)
    near_in[near_id] = near_src[near_id]

    def solve_chunk(x, carry):
        rows = chunk_rows(x)
        field = jnp.concatenate(to_modes(vectors, layers_of(residual[rows])), axis=0)
        field = row_operator(v_row[2], field)
        field = lane_operator(v_lane[2], field) * v_fdm[rows]
        field = lane_operator(v_lane[3], field)
        field = row_operator(v_row[3], field)
        correction[rows] = jnp.concatenate(from_modes(vectors, layers_of(field)), axis=0)
        return carry

    third = ex // 2
    lax.fori_loop(0, third, solve_chunk, 0)

    await_exchange(0, lay.pack, near_in, sum_recv)
    far_in[far_id] = jnp.sum(near_in[...], axis=0)
    exchange(1, lay.far, far_id, far_device, lambda index: far_in.at[far_id], far_in)

    lax.fori_loop(third, ex, solve_chunk, 0)
    second_copies = send_faces(correction, 1)

    await_exchange(1, lay.far, far_in, sum_recv)
    full_in[near_id] = jnp.sum(far_in[...], axis=0)
    exchange(2, lay.pack, near_id, near_device, lambda index: full_in.at[near_id], full_in)

    join_faces(correction, 1, second_copies)

    await_exchange(2, lay.pack, full_in, sum_recv)

    def value_block(index, total):
        for k in range(lay.share):
            line = index * lay.share + k
            value = jnp.broadcast_to(full_in[index, pl.ds(k, 1)], (columns, lanes))
            total = total + v_fac[:, pl.ds(pl.multiple_of(line * lanes, lanes), lanes)] * value
        return total

    totals = lax.fori_loop(0, lay.pack, value_block, jnp.zeros((columns, lanes), jnp.float32))
    values = jnp.broadcast_to(jnp.sum(totals, axis=1, keepdims=True), (columns, lanes))
    own_coarse[...] = values.reshape(ex, ey, lanes)

    ring_copies = []
    for index, (g, d) in enumerate(steps):
        x = 0 if g < 0 else ex - 1
        if d == 0:
            source, target = own_coarse.at[x], ring_x.at[(1 - g) // 2]
        elif g == 0:
            source, target = own_coarse, ring_y.at[(1 - d) // 2]
        else:
            source, target = own_coarse.at[x], ring_d.at[(1 - g) // 2, (1 - d) // 2]
        copy = pltpu.make_async_remote_copy(
            src_ref=source,
            dst_ref=target,
            send_sem=ring_send.at[index],
            recv_sem=ring_recv.at[index],
            device_id=neighbour(g, d),
            device_id_type=MESH_IDS,
        )
        copy.start()
        ring_copies.append(copy)
    for copy in ring_copies:
        copy.wait_recv()

    def padded(inside, below, above):
        return [low_g * below] + inside + [high_g * above]

    center = padded([own_coarse[x] for x in range(ex)], ring_x[0], ring_x[1])
    left = padded([ring_y[0, x] for x in range(ex)], ring_d[0, 0], ring_d[1, 0])
    right = padded([ring_y[1, x] for x in range(ex)], ring_d[0, 1], ring_d[1, 1])
    twice = 1.0 + shared
    for x in range(ex):
        rows = x * chunk
        for part in range(3):
            def joined(values):
                value = values[x + 1]
                if part == 0:
                    value = value + values[x]
                elif part == 2:
                    value = value + values[x + 2]
                return value * twice

            inside = joined(center)
            before = low_d * pltpu.roll(joined(left), 1, axis=0)
            after = high_d * pltpu.roll(joined(right), ey - 1, axis=0)
            below = jnp.where(first_line, before, pltpu.roll(inside, 1, axis=0))
            above = jnp.where(last_line, after, pltpu.roll(inside, ey - 1, axis=0))
            for j in range(n):
                value = inside
                if j == 0:
                    value = inside + below
                elif j == n - 1:
                    value = inside + above
                coarse_tile[part, pl.ds(j, ey, stride=n)] = value
            layers = {0: [0], 1: list(range(1, n - 1)), 2: [n - 1]}[part]
            tile = coarse_tile[part]
            for layer in layers:
                spot = pl.ds(rows + layer * slab, slab)
                correction[spot] = correction[spot] + tile

    for copy in first_copies + second_copies + ring_copies:
        copy.wait_send()
    await_exchange(0, lay.pack, near_in, sum_send)
    await_exchange(1, lay.far, far_in, sum_send)
    await_exchange(2, lay.pack, full_in, sum_send)


def solution(mesh):
    groups, devices = mesh.shape["grp"], mesh.shape["dev"]

    def body(adjoint, right_side, velocity, conductivity, mass_term, fdm_inverse, coarse_factor):
        ex, n, ey, _, lanes = adjoint.shape
        lay = Layout(ex, n, ey, lanes, groups, devices, coarse_factor.shape[1])
        derivative, vectors, lane_tables, row_tables = operator_tables(n, lanes)
        flat = (lay.rows, lanes)
        f32, bf16 = jnp.float32, jnp.bfloat16
        anywhere = pl.BlockSpec(memory_space=pltpu.HBM)
        vmem = pl.BlockSpec(memory_space=pltpu.VMEM)
        scratch = [
            pltpu.VMEM(flat, f32),
            pltpu.VMEM(flat, f32),
            pltpu.VMEM((3,) + flat, f32),
            pltpu.VMEM(flat, f32),
            pltpu.VMEM(flat, f32),
            pltpu.VMEM(flat, f32),
            pltpu.VMEM(coarse_factor.shape, f32),
            pltpu.VMEM(lane_tables.shape, bf16),
            pltpu.VMEM(row_tables.shape, bf16),
            pltpu.VMEM(flat, f32),
            pltpu.VMEM((2, 2, lay.slab, lanes), f32),
            pltpu.VMEM((2, 2, lay.slab, lanes), f32),
            pltpu.VMEM((2, 2, ex, n, lanes), f32),
            pltpu.VMEM((2, 2, ex, n, lanes), f32),
            pltpu.VMEM((2, 2, 2, n, lanes), f32),
            pltpu.VMEM((lay.lines * ey, lanes), f32),
            pltpu.VMEM((ex * lay.slab, lanes), f32),
            pltpu.VMEM((lay.coarse_lines * 8, lanes), f32),
            pltpu.VMEM((lay.pack, lay.share, lanes), f32),
            pltpu.VMEM((lay.pack, lay.share, lanes), f32),
            pltpu.VMEM((lay.far, lay.share, lanes), f32),
            pltpu.VMEM((lay.pack, lay.share, lanes), f32),
            pltpu.VMEM((ex, ey, lanes), f32),
            pltpu.VMEM((2, ey, lanes), f32),
            pltpu.VMEM((2, ex, ey, lanes), f32),
            pltpu.VMEM((2, 2, ey, lanes), f32),
            pltpu.VMEM((8, lanes), f32),
            pltpu.VMEM((3, lay.slab, lanes), f32),
            pltpu.SemaphoreType.DMA((6, 4)),
            pltpu.SemaphoreType.DMA((2, 8)),
            pltpu.SemaphoreType.DMA((2, 8)),
            pltpu.SemaphoreType.DMA((8,)),
            pltpu.SemaphoreType.DMA((8,)),
            pltpu.SemaphoreType.DMA((3,)),
            pltpu.SemaphoreType.DMA((3,)),
        ]
        residual, correction = pl.pallas_call(
            functools.partial(step_kernel, lay, derivative, vectors),
            out_shape=[jax.ShapeDtypeStruct(flat, f32)] * 2,
            in_specs=[anywhere] * 9,
            out_specs=[vmem, vmem],
            scratch_shapes=scratch,
            compiler_params=pltpu.CompilerParams(
                collective_id=0, has_side_effects=True, vmem_limit_bytes=40 * 1024 * 1024
            ),
            name="adjoint_step",
        )(
            *[
                pltpu.with_memory_space_constraint(array, pltpu.HBM)
                for array in (
                    adjoint.reshape(flat),
                    right_side.reshape(flat),
                    velocity.reshape((3,) + flat),
                    conductivity.reshape(flat),
                    mass_term.reshape(flat),
                    fdm_inverse.reshape(flat),
                    coarse_factor,
                    jnp.asarray(lane_tables),
                    jnp.asarray(row_tables),
                )
            ]
        )
        return residual.reshape(adjoint.shape), correction.reshape(adjoint.shape)

    field = P("grp", None, "dev", None, None)
    in_specs = (
        field,
        field,
        P(None, "grp", None, "dev", None, None),
        field,
        field,
        field,
        P(("grp", "dev"), None),
    )
    return jax.shard_map(
        body, mesh=mesh, in_specs=in_specs, out_specs=(field, field), check_vma=False
    )
```

```python
import functools
import math

import jax
import jax.numpy as jnp
import ml_dtypes
import numpy as np
from jax import lax
from jax.experimental import pallas as pl
from jax.experimental.pallas import tpu as pltpu
from jax.sharding import PartitionSpec as P

GLL_POINTS = [
    -1.0,
    -0.871740148509607,
    -0.591700181433142,
    -0.209299217902479,
    0.209299217902479,
    0.591700181433142,
    0.871740148509607,
    1.0,
]


def legendre_value(point, highest):
    previous = 1.0
    current = point
    for degree in range(1, highest):
        previous, current = (
            current,
            ((2 * degree + 1) * point * current - degree * previous) / (degree + 1),
        )
    return current


def identity_list(dimension):
    return [
        [1.0 if row_index == col_index else 0.0 for col_index in range(dimension)]
        for row_index in range(dimension)
    ]


def transpose_list(matrix):
    return [
        [matrix[row_index][col_index] for row_index in range(len(matrix))]
        for col_index in range(len(matrix[0]))
    ]


def matrix_product(left, right):
    inner_size = len(right)
    return [
        [
            sum((left[row_index][inner] * right[inner][col_index] for inner in range(inner_size)))
            for col_index in range(len(right[0]))
        ]
        for row_index in range(len(left))
    ]


def jacobi_eigen(matrix):
    current = [list(line) for line in matrix]
    dimension = len(matrix)
    rotations = identity_list(dimension)
    for repeat in range(12):
        for row_index in range(dimension - 1):
            for col_index in range(row_index + 1, dimension):
                angle = 0.5 * math.atan2(
                    2.0 * current[row_index][col_index],
                    current[row_index][row_index] - current[col_index][col_index],
                )
                cosine = math.cos(angle)
                sine_value = math.sin(angle)
                rotation = identity_list(dimension)
                rotation[row_index][row_index] = cosine
                rotation[col_index][col_index] = cosine
                rotation[row_index][col_index] = -sine_value
                rotation[col_index][row_index] = sine_value
                current = matrix_product(
                    matrix_product(transpose_list(rotation), current), rotation
                )
                rotations = matrix_product(rotations, rotation)
    ordering = sorted(range(dimension), key=lambda position: current[position][position])
    return [
        [rotations[row_index][position] for position in ordering] for row_index in range(dimension)
    ]


def element_tables():
    total_points = len(GLL_POINTS)
    weights_bary = []
    for row_index in range(total_points):
        product_value = 1.0
        for col_index in range(total_points):
            if col_index != row_index:
                product_value = product_value * (GLL_POINTS[row_index] - GLL_POINTS[col_index])
        weights_bary.append(1.0 / product_value)
    derivative = [[0.0] * total_points for row_index in range(total_points)]
    for row_index in range(total_points):
        for col_index in range(total_points):
            if col_index != row_index:
                derivative[row_index][col_index] = (
                    weights_bary[col_index]
                    / weights_bary[row_index]
                    / (GLL_POINTS[row_index] - GLL_POINTS[col_index])
                )
        derivative[row_index][row_index] = -sum(derivative[row_index])
    quadrature = [
        2.0 / ((total_points - 1) * total_points * legendre_value(point, total_points - 1) ** 2)
        for point in GLL_POINTS
    ]
    stiffness = [
        [
            sum(
                (
                    derivative[inner][row_index] * quadrature[inner] * derivative[inner][col_index]
                    for inner in range(total_points)
                )
            )
            + (quadrature[row_index] if row_index == col_index else 0.0)
            for col_index in range(total_points)
        ]
        for row_index in range(total_points)
    ]
    return (derivative, jacobi_eigen(stiffness))


def block_diagonal(blocks, matrix):
    node_count = len(matrix)
    total = blocks * node_count
    return [
        [
            (
                matrix[row_index % node_count][col_index % node_count]
                if row_index // node_count == col_index // node_count
                else 0.0
            )
            for col_index in range(total)
        ]
        for row_index in range(total)
    ]


def assembly_table(blocks, node_count):
    total = blocks * node_count
    shared_index = [
        position // node_count * (node_count - 1) + position % node_count
        for position in range(total)
    ]
    return [
        [
            1.0 if shared_index[row_index] == shared_index[col_index] else 0.0
            for col_index in range(total)
        ]
        for row_index in range(total)
    ]

MESH_IDS = pl.DeviceIdType.MESH
TILE = 128
PACK = 16


def split_halves(values):
    high = values.astype(jnp.bfloat16)
    return high, (values - high.astype(jnp.float32)).astype(jnp.bfloat16)


def lane_operator(table, field):
    high, low = split_halves(field)
    stacked = jnp.concatenate([table, table], axis=0)
    product = jnp.dot(
        jnp.concatenate([high, low], axis=1), stacked, preferred_element_type=jnp.float32
    )
    return product[:, :TILE] + product[:, TILE:]


def row_operator(table, field):
    high, low = split_halves(field)
    stacked = jnp.concatenate([table, table], axis=1)
    results = []
    for start in range(0, field.shape[0], 2 * TILE):
        first, second = slice(start, start + TILE), slice(start + TILE, start + 2 * TILE)
        operand = jnp.concatenate(
            [
                jnp.concatenate([high[first], low[first]], axis=0),
                jnp.concatenate([high[second], low[second]], axis=0),
            ],
            axis=1,
        )
        product = jnp.dot(stacked, operand, preferred_element_type=jnp.float32)
        summed = product[:TILE] + product[TILE:]
        results += [summed[:, :TILE], summed[:, TILE:]]
    return jnp.concatenate(results, axis=0)


def weighted(coefficients, terms):
    total = terms[0] * coefficients[0]
    for coefficient, term in zip(coefficients[1:], terms[1:]):
        total = total + term * coefficient
    return total


def mirrored(layers):
    count = len(layers)
    half = count // 2
    sums = [layers[k] + layers[count - 1 - k] for k in range(half)]
    gaps = [layers[k] - layers[count - 1 - k] for k in range(half)]
    return sums, gaps


def odd_operator(matrix, layers):
    count = len(layers)
    half = count // 2
    sums, gaps = mirrored(layers)
    lower, upper = [], []
    for row in range(half):
        line = matrix[row]
        even = weighted([0.5 * (line[k] + line[count - 1 - k]) for k in range(half)], sums)
        odd = weighted([0.5 * (line[k] - line[count - 1 - k]) for k in range(half)], gaps)
        lower.append(odd + even)
        upper.append(odd - even)
    return lower + upper[::-1]


def to_modes(vectors, layers):
    count = len(layers)
    half = count // 2
    sums, gaps = mirrored(layers)
    return [
        weighted([vectors[k][mode] for k in range(half)], gaps if mode % 2 else sums)
        for mode in range(count)
    ]


def from_modes(vectors, modes):
    count = len(modes)
    half = count // 2
    lower, upper = [], []
    for row in range(half):
        even = weighted(vectors[row][0::2], modes[0::2])
        odd = weighted(vectors[row][1::2], modes[1::2])
        lower.append(even + odd)
        upper.append(even - odd)
    return lower + upper[::-1]


def half_pair(matrix):
    table = np.asarray(matrix, np.float64).astype(np.float32)
    high = table.astype(ml_dtypes.bfloat16)
    low = (table - high.astype(np.float32)).astype(ml_dtypes.bfloat16)
    return high, low


def lane_table(matrix):
    return np.concatenate(half_pair(matrix), axis=1)


def row_table(matrix):
    return np.concatenate(half_pair(matrix), axis=0)


def operator_tables(nodes, lanes):
    derivative, vectors = element_tables()
    blocks = lanes // nodes
    backward_z = block_diagonal(blocks, derivative)
    vectors_z = block_diagonal(blocks, vectors)
    joined = assembly_table(blocks, nodes)
    physical_joined = (np.asarray(transpose_list(vectors_z)) @ np.asarray(joined)).tolist()
    lane_tables = np.stack(
        [
            lane_table(transpose_list(backward_z)),
            lane_table(backward_z),
            lane_table(vectors_z),
            lane_table(physical_joined),
        ]
    )
    row_tables = np.stack(
        [
            row_table(backward_z),
            row_table(transpose_list(backward_z)),
            row_table(transpose_list(vectors_z)),
            row_table(vectors_z),
        ]
    )
    return derivative, vectors, lane_tables, row_tables


class Layout:
    def __init__(self, elements_x, nodes, elements_y, lanes, groups, devices, coarse):
        self.ex, self.n, self.ey, self.lanes = elements_x, nodes, elements_y, lanes
        self.groups, self.devices = groups, devices
        self.slab = elements_y * nodes
        self.chunk = nodes * self.slab
        self.rows = elements_x * self.chunk
        self.lines = elements_x * nodes
        self.columns = elements_x * elements_y
        self.pack = math.gcd(PACK, devices)
        self.far = groups * (devices // self.pack)
        self.coarse = coarse
        self.coarse_lines = coarse // lanes
        self.share = self.coarse_lines // self.pack


def step_kernel(
    lay, derivative, vectors,
    adjoint, right_side, velocity, conductivity, mass_term, fdm_inverse, factor, lane_t, row_t,
    residual, correction, grid,
    v_adj, v_rs, v_vel, v_con, v_mass, v_fdm, v_fac, v_lane, v_row,
    local, side_send, side_recv, row_send, row_recv, edge_recv, halo_lines,
    column_sum, inner_part, near_src, near_in, far_in, full_in,
    sum_tile, note_send, note_recv, rim_send, rim_recv, ring_out, ring_in,
    load_sem, face_send, face_recv, note_sent, note_got, rim_sem, ring_sem, sum_send, sum_recv,
):
    ex, n, ey, lanes = lay.ex, lay.n, lay.ey, lay.lanes
    slab, chunk, lines, columns = lay.slab, lay.chunk, lay.lines, lay.columns
    group = lax.axis_index("grp")
    device = lax.axis_index("dev")
    near_id = lax.rem(device, lay.pack)
    block_id = device // lay.pack
    far_blocks = lay.devices // lay.pack
    far_id = group * far_blocks + block_id

    def near_device(index):
        return (group, block_id * lay.pack + index)

    def far_device(index):
        return (index // far_blocks, lax.rem(index, far_blocks) * lay.pack + near_id)

    def neighbour(step_g, step_d):
        return (
            lax.rem(group + step_g + lay.groups, lay.groups),
            lax.rem(device + step_d + lay.devices, lay.devices),
        )

    steps = [(g, d) for g in (-1, 0, 1) for d in (-1, 0, 1) if (g, d) != (0, 0)]

    def chunk_rows(x):
        return pl.ds(pl.multiple_of(x * chunk, chunk), chunk)

    def chunk_loads(x):
        rows = chunk_rows(x)
        return [
            pltpu.make_async_copy(adjoint.at[rows], v_adj.at[rows], load_sem.at[0, x]),
            pltpu.make_async_copy(conductivity.at[rows], v_con.at[rows], load_sem.at[1, x]),
            pltpu.make_async_copy(velocity.at[:, rows], v_vel.at[:, rows], load_sem.at[2, x]),
            pltpu.make_async_copy(mass_term.at[rows], v_mass.at[rows], load_sem.at[3, x]),
        ]

    def table_loads(part):
        half = pl.ds(2 * part, 2)
        return [
            pltpu.make_async_copy(lane_t.at[half], v_lane.at[half], load_sem.at[4 + part, 0]),
            pltpu.make_async_copy(row_t.at[half], v_row.at[half], load_sem.at[4 + part, 1]),
        ]

    late_loads = [
        pltpu.make_async_copy(right_side, v_rs, load_sem.at[4, 2]),
        pltpu.make_async_copy(factor, v_fac, load_sem.at[4, 3]),
        pltpu.make_async_copy(fdm_inverse, v_fdm, load_sem.at[5, 2]),
    ] + table_loads(1)
    for copy in chunk_loads(0) + table_loads(0):
        copy.start()

    barrier = pltpu.get_barrier_semaphore()
    for step in steps:
        pl.semaphore_signal(barrier, inc=1, device_id=neighbour(*step), device_id_type=MESH_IDS)
    for offset in range(1, lay.pack):
        target = near_device(lax.rem(near_id + offset, lay.pack))
        pl.semaphore_signal(barrier, inc=1, device_id=target, device_id_type=MESH_IDS)
    for offset in range(1, lay.far):
        target = far_device(lax.rem(far_id + offset, lay.far))
        pl.semaphore_signal(barrier, inc=1, device_id=target, device_id_type=MESH_IDS)


    lane_index = lax.broadcasted_iota(jnp.int32, (1, lanes), 1)
    lane_node = lax.rem(lane_index, n)
    is_upper = lane_node == n - 1
    shared = jnp.where(
        (is_upper & (lane_index != lanes - 1)) | ((lane_node == 0) & (lane_index != 0)), 1.0, 0.0
    ).astype(jnp.float32)
    line_index = lax.broadcasted_iota(jnp.int32, (n, lanes), 0)
    first_line = line_index == 0
    last_line = line_index == n - 1

    for copy in chunk_loads(1):
        copy.start()

    def layers_of(field):
        return [field[k * slab : (k + 1) * slab] for k in range(n)]

    def load_chunk(x):
        for copy in chunk_loads(x) + (table_loads(0) if x == 0 else []):
            copy.wait()
        if x + 2 < ex:
            for copy in chunk_loads(x + 2):
                copy.start()
        elif x + 2 == ex:
            late_loads[0].start()
        else:
            for copy in late_loads[1:]:
                copy.start()

    def fluxes(x):
        rows = pl.ds(x * chunk, chunk)
        field = v_adj[rows]
        diffusion = v_con[rows]
        third = diffusion * lane_operator(v_lane[0], field) + v_vel[2, rows] * field
        second = diffusion * row_operator(v_row[0], field) + v_vel[1, rows] * field
        gradient = jnp.concatenate(odd_operator(derivative, layers_of(field)), axis=0)
        first = diffusion * gradient + v_vel[0, rows] * field
        return first, second, third

    def divergence(x, first, second, third):
        rows = pl.ds(x * chunk, chunk)
        total = lane_operator(v_lane[1], third) + row_operator(v_row[1], second)
        total = total + jnp.concatenate(
            odd_operator(transpose_list(derivative), layers_of(first)), axis=0
        )
        total = total + v_mass[rows] * v_adj[rows]
        crossed = jnp.where(
            is_upper, pltpu.roll(total, lanes - 1, axis=1), pltpu.roll(total, 1, axis=1)
        )
        local[rows] = total + shared * crossed

    earlier = None
    for x in range(ex):
        load_chunk(x)
        current = fluxes(x)
        if x > 0:
            divergence(x - 1, *earlier)
        earlier = current
    divergence(ex - 1, *earlier)

    low_g = jnp.where(group > 0, 1.0, 0.0).astype(jnp.float32)
    high_g = jnp.where(group < lay.groups - 1, 1.0, 0.0).astype(jnp.float32)
    low_d = jnp.where(device > 0, 1.0, 0.0).astype(jnp.float32)
    high_d = jnp.where(device < lay.devices - 1, 1.0, 0.0).astype(jnp.float32)
    gates_g, gates_d = (low_g, high_g), (low_d, high_d)

    def face_copies(phase):
        copies = []
        for index, (g, d) in enumerate(steps):
            if d == 0:
                source, target = side_send.at[phase, (g + 1) // 2], side_recv.at[phase, (1 - g) // 2]
            elif g == 0:
                source, target = row_send.at[phase, (d + 1) // 2], row_recv.at[phase, (1 - d) // 2]
            else:
                x = 0 if g < 0 else ex - 1
                source = row_send.at[phase, (d + 1) // 2, x]
                target = edge_recv.at[phase, (1 - g) // 2, (1 - d) // 2]
            copies.append(
                pltpu.make_async_remote_copy(
                    src_ref=source,
                    dst_ref=target,
                    send_sem=face_send.at[phase, index],
                    recv_sem=face_recv.at[phase, index],
                    device_id=neighbour(g, d),
                    device_id_type=MESH_IDS,
                )
            )
        return copies

    def pack_faces(field, phase):
        side_send[phase, 0] = field[pl.ds(0, slab)]
        side_send[phase, 1] = field[pl.ds(lay.rows - slab, slab)]
        for x in range(ex - 1):
            upper, lower = pl.ds((x + 1) * chunk - slab, slab), pl.ds((x + 1) * chunk, slab)
            both = field[upper] + field[lower]
            field[upper] = both
            field[lower] = both
        for x in range(ex):
            row_send[phase, 0, x] = field[pl.ds(x * chunk, n, stride=slab)]
            row_send[phase, 1, x] = field[pl.ds(x * chunk + slab - 1, n, stride=slab)]

    def send_faces(phase):
        copies = face_copies(phase)
        for copy in copies:
            copy.start()
        return copies

    def join_faces(field, phase, copies):
        for copy in copies:
            copy.wait_recv()
        head, tail = pl.ds(0, slab), pl.ds(lay.rows - slab, slab)
        field[head] = field[head] + low_g * side_recv[phase, 0]
        field[tail] = field[tail] + high_g * side_recv[phase, 1]
        for d in range(2):
            low_edge = edge_recv[phase, 0, d, pl.ds(n - 1, n, stride=0)]
            high_edge = edge_recv[phase, 1, d, pl.ds(0, n, stride=0)]
            first = row_recv[phase, d, 0] + jnp.where(first_line, low_g * low_edge, 0.0)
            row_recv[phase, d, 0] = first
            last = row_recv[phase, d, ex - 1] + jnp.where(last_line, high_g * high_edge, 0.0)
            row_recv[phase, d, ex - 1] = last
            spot = 0 if d == 0 else n - 1
            for x in range(ex):
                halo_lines[pl.ds(x * slab + spot, n, stride=n)] = gates_d[d] * row_recv[phase, d, x]
        starts = pl.ds(0, lines * ey, stride=n)
        ends = pl.ds(n - 1, lines * ey, stride=n)
        lower = field[starts].reshape(lines, ey, lanes)
        upper = field[ends].reshape(lines, ey, lanes)
        outside = halo_lines[...].reshape(lines, ey, lanes)
        from_below = jnp.where(first_line, outside, pltpu.roll(upper, 1, axis=1))
        from_above = jnp.where(last_line, outside, pltpu.roll(lower, ey - 1, axis=1))
        field[starts] = (lower + from_below).reshape(lines * ey, lanes)
        field[ends] = (upper + from_above).reshape(lines * ey, lanes)

    def line_sum(start):
        total = column_sum[pl.ds(start, ey, stride=n)]
        for j in range(1, n):
            total = total + column_sum[pl.ds(start + j, ey, stride=n)]
        return total

    def joined_sum(start):
        lower = column_sum[pl.ds(start, ey, stride=n)]
        upper = column_sum[pl.ds(start + n - 1, ey, stride=n)]
        below = jnp.where(first_line, 0.0, pltpu.roll(upper, 1, axis=0))
        above = jnp.where(last_line, 0.0, pltpu.roll(lower, ey - 1, axis=0))
        return line_sum(start) + below + above

    pack_faces(local, 0)
    for side in range(2):
        column_sum[pl.ds(side * slab, slab)] = side_send[0, side]
    for side in range(2):
        note_send[side] = joined_sum(side * slab)
    base = 2 * slab
    for x in range(ex):
        layers = layers_of(local[pl.ds(x * chunk, chunk)])
        total = layers[0]
        for layer in layers[1:]:
            total = total + layer
        column_sum[pl.ds(base + x * slab, slab)] = total
    for x in range(ex):
        start = base + x * slab
        sum_tile[x] = joined_sum(start)
        note_send[2, pl.ds(x, 1)] = column_sum[pl.ds(start, 1)]
        note_send[3, pl.ds(x, 1)] = column_sum[pl.ds(start + slab - 1, 1)]
    for side_g in range(2):
        for side_d in range(2):
            spot = side_g * slab + side_d * (slab - 1)
            note_send[4 + 2 * side_g + side_d] = jnp.broadcast_to(
                column_sum[pl.ds(spot, 1)], (ey, lanes)
            )
    def note_slot(g, d):
        if d == 0:
            return (g + 1) // 2
        if g == 0:
            return 2 + (d + 1) // 2
        return 4 + 2 * ((g + 1) // 2) + (d + 1) // 2

    note_copies = [
        pltpu.make_async_remote_copy(
            src_ref=note_send.at[note_slot(g, d)],
            dst_ref=note_recv.at[note_slot(-g, -d)],
            send_sem=note_sent.at[index],
            recv_sem=note_got.at[index],
            device_id=neighbour(g, d),
            device_id_type=MESH_IDS,
        )
        for index, (g, d) in enumerate(steps)
    ]

    pl.semaphore_wait(barrier, len(steps) + lay.pack - 1 + lay.far - 1)
    for copy in note_copies:
        copy.start()
    first_copies = send_faces(0)
    late_loads[0].wait()
    for x in range(ex):
        layers = layers_of(v_rs[pl.ds(x * chunk, chunk)])
        total = layers[0]
        for layer in layers[1:]:
            total = total + layer
        column_sum[pl.ds(x * slab, slab)] = total
    for x in range(ex):
        sum_tile[x] = line_sum(x * slab) - sum_tile[x]
    late_loads[1].wait()
    def rim_block(line, carry):
        spot = pl.ds(pl.multiple_of(line * lanes, lanes), lanes)
        for x in range(ex):
            rim_send[0, line, pl.ds(x, 1)] = v_fac[pl.ds(x * ey, 1), spot]
            rim_send[1, line, pl.ds(x, 1)] = v_fac[pl.ds(x * ey + ey - 1, 1), spot]
        return carry

    lax.fori_loop(0, lay.coarse_lines, rim_block, 0)

    rim_copies = [
        pltpu.make_async_remote_copy(
            src_ref=rim_send.at[(d + 1) // 2],
            dst_ref=rim_recv.at[(1 - d) // 2],
            send_sem=rim_sem.at[0, (d + 1) // 2],
            recv_sem=rim_sem.at[1, (d + 1) // 2],
            device_id=neighbour(0, d),
            device_id_type=MESH_IDS,
        )
        for d in (-1, 1)
    ]
    for copy in rim_copies:
        copy.start()
    for copy in note_copies:
        copy.wait_recv()
    sums = []
    for x in range(ex):
        total = sum_tile[x]
        ends = []
        for d in range(2):
            end = note_recv[2 + d, pl.ds(x, ey, stride=0)]
            if x == 0:
                end = end + low_g * note_recv[4 + d]
            if x == ex - 1:
                end = end + high_g * note_recv[6 + d]
            ends.append(gates_d[d] * end)
        if x == 0:
            total = total - low_g * note_recv[0]
        if x == ex - 1:
            total = total - high_g * note_recv[1]
        total = total - jnp.where(first_line, ends[0], 0.0) - jnp.where(last_line, ends[1], 0.0)
        sums.append(total)
    means = jnp.sum(jnp.concatenate(sums, axis=0), axis=1, keepdims=True)
    means = jnp.broadcast_to(means * (1.0 / float(n * n * lanes)), (columns, lanes))

    def inner_block(block, carry):
        for k in range(8):
            line = block * 8 + k
            piece = v_fac[:, pl.ds(pl.multiple_of(line * lanes, lanes), lanes)] * means
            total = piece[0:8]
            for start in range(8, columns, 8):
                total = total + piece[start : start + 8]
            inner_part[pl.ds(pl.multiple_of(line * 8, 8), 8)] = total
        return carry

    lax.fori_loop(0, lay.coarse_lines // 8, inner_block, 0)
    for index in range(lay.pack):
        base = index * lay.share * 8
        total = inner_part[pl.ds(base, lay.share, stride=8)]
        for k in range(1, 8):
            total = total + inner_part[pl.ds(base + k, lay.share, stride=8)]
        near_src[index] = total

    def exchange(stage, count, own, device_of, source_of, buffer):
        def send(offset, carry):
            index = lax.rem(own + offset, count)
            pltpu.make_async_remote_copy(
                src_ref=source_of(index),
                dst_ref=buffer.at[own],
                send_sem=sum_send.at[stage],
                recv_sem=sum_recv.at[stage],
                device_id=device_of(index),
                device_id_type=MESH_IDS,
            ).start()
            return carry

        for offset in range(1, count):
            send(offset, 0)

    def await_exchange(stage, count, buffer, sem):
        part = buffer.at[pl.ds(0, count - 1)]
        pltpu.make_async_copy(part, part, sem.at[stage]).wait()

    exchange(0, lay.pack, near_id, near_device, lambda index: near_src.at[index], near_in)
    near_in[near_id] = near_src[near_id]

    join_faces(local, 0, first_copies)
    for x in range(ex):
        rows = pl.ds(x * chunk, chunk)
        residual[rows] = v_rs[rows] - local[rows]

    for copy in late_loads[2:]:
        copy.wait()

    def solve_chunk(x):
        rows = pl.ds(x * chunk, chunk)
        field = jnp.concatenate(to_modes(vectors, layers_of(residual[rows])), axis=0)
        field = row_operator(v_row[2], field)
        field = lane_operator(v_lane[2], field) * v_fdm[rows]
        field = lane_operator(v_lane[3], field)
        field = row_operator(v_row[3], field)
        correction[rows] = jnp.concatenate(from_modes(vectors, layers_of(field)), axis=0)

    for x in range(ex // 2):
        solve_chunk(x)

    await_exchange(0, lay.pack, near_in, sum_recv)
    far_in[far_id] = jnp.sum(near_in[...], axis=0)
    exchange(1, lay.far, far_id, far_device, lambda index: far_in.at[far_id], far_in)

    for x in range(ex // 2, ex):
        solve_chunk(x)
    pack_faces(correction, 1)
    second_copies = send_faces(1)

    await_exchange(1, lay.far, far_in, sum_recv)
    full_in[near_id] = jnp.sum(far_in[...], axis=0)
    exchange(2, lay.pack, near_id, near_device, lambda index: full_in.at[near_id], full_in)

    for copy in rim_copies:
        copy.wait_recv()

    await_exchange(2, lay.pack, full_in, sum_recv)

    def value_block(index, totals):
        inside, left, right = totals
        for k in range(lay.share):
            line = index * lay.share + k
            value = jnp.broadcast_to(full_in[index, pl.ds(k, 1)], (columns, lanes))
            spot = pl.ds(pl.multiple_of(line * lanes, lanes), lanes)
            inside = inside + v_fac[:, spot] * value
            left = left + rim_recv[0, line] * value[:ex]
            right = right + rim_recv[1, line] * value[:ex]
        return inside, left, right

    none = jnp.zeros((ex, lanes), jnp.float32)
    inside, left, right = lax.fori_loop(
        0, lay.pack, value_block, (jnp.zeros((columns, lanes), jnp.float32), none, none)
    )
    inside = jnp.broadcast_to(jnp.sum(inside, axis=1, keepdims=True), (columns, lanes))
    left = low_d * jnp.sum(left, axis=1, keepdims=True)
    right = high_d * jnp.sum(right, axis=1, keepdims=True)
    for x in range(ex):
        grid[0, 1 + x] = inside[x * ey : (x + 1) * ey]
        grid[1, 1 + x] = jnp.broadcast_to(left[x : x + 1], (ey, lanes))
        grid[2, 1 + x] = jnp.broadcast_to(right[x : x + 1], (ey, lanes))
    for part in range(3):
        ring_out[0, part] = grid[part, 1]
        ring_out[1, part] = grid[part, ex]
    ring_copies = [
        pltpu.make_async_remote_copy(
            src_ref=ring_out.at[(g + 1) // 2],
            dst_ref=ring_in.at[(1 - g) // 2],
            send_sem=ring_sem.at[0, (g + 1) // 2],
            recv_sem=ring_sem.at[1, (g + 1) // 2],
            device_id=neighbour(g, 0),
            device_id_type=MESH_IDS,
        )
        for g in (-1, 1)
    ]
    for copy in ring_copies:
        copy.start()
    join_faces(correction, 1, second_copies)
    for copy in ring_copies:
        copy.wait_recv()
    for part in range(3):
        grid[part, 0] = low_g * ring_in[0, part]
        grid[part, ex + 1] = high_g * ring_in[1, part]

    for copy in note_copies + first_copies + rim_copies + second_copies + ring_copies:
        copy.wait_send()
    await_exchange(0, lay.pack, near_in, sum_send)
    await_exchange(1, lay.far, far_in, sum_send)
    await_exchange(2, lay.pack, full_in, sum_send)


def finish_kernel(lay, residual, solved, grid, out_residual, out_correction, staged, tile, sem):
    ex, n, ey, lanes, slab, chunk = lay.ex, lay.n, lay.ey, lay.lanes, lay.slab, lay.chunk
    copies = [pltpu.make_async_copy(residual, out_residual, sem.at[0])]
    copies[0].start()
    lane_index = lax.broadcasted_iota(jnp.int32, (1, lanes), 1)
    lane_node = lax.rem(lane_index, n)
    shared = ((lane_node == n - 1) & (lane_index != lanes - 1)) | (
        (lane_node == 0) & (lane_index != 0)
    )
    copies_of = jnp.where(shared, 2.0, 1.0).astype(jnp.float32)
    line_index = lax.broadcasted_iota(jnp.int32, (ey, lanes), 0)
    first_line, last_line = line_index == 0, line_index == ey - 1
    for x in range(ex):
        for part in range(3):
            sides = []
            for side in range(3):
                value = grid[side, x + 1]
                if part == 0:
                    value = value + grid[side, x]
                elif part == 2:
                    value = value + grid[side, x + 2]
                sides.append(value * copies_of)
            inside, left, right = sides
            below = jnp.where(first_line, left, pltpu.roll(inside, 1, axis=0))
            above = jnp.where(last_line, right, pltpu.roll(inside, ey - 1, axis=0))
            for j in range(n):
                value = inside
                if j == 0:
                    value = inside + below
                elif j == n - 1:
                    value = inside + above
                tile[x, part, pl.ds(j, ey, stride=n)] = value
        for layer in range(n):
            part = 0 if layer == 0 else 2 if layer == n - 1 else 1
            spot = pl.ds(x * chunk + layer * slab, slab)
            staged[spot] = solved[spot] + tile[x, part]
        rows = pl.ds(x * chunk, chunk)
        copy = pltpu.make_async_copy(staged.at[rows], out_correction.at[rows], sem.at[1 + x])
        copy.start()
        copies.append(copy)
    for copy in copies:
        copy.wait()


def solution(mesh):
    groups, devices = mesh.shape["grp"], mesh.shape["dev"]

    def body(adjoint, right_side, velocity, conductivity, mass_term, fdm_inverse, coarse_factor):
        ex, n, ey, _, lanes = adjoint.shape
        lay = Layout(ex, n, ey, lanes, groups, devices, coarse_factor.shape[1])
        derivative, vectors, lane_tables, row_tables = operator_tables(n, lanes)
        flat = (lay.rows, lanes)
        f32, bf16 = jnp.float32, jnp.bfloat16
        hbm = pl.BlockSpec(memory_space=pltpu.HBM)
        vmem = pl.BlockSpec(memory_space=pltpu.VMEM)
        scratch = [
            pltpu.VMEM(flat, f32),
            pltpu.VMEM(flat, f32),
            pltpu.VMEM((3,) + flat, f32),
            pltpu.VMEM(flat, f32),
            pltpu.VMEM(flat, f32),
            pltpu.VMEM(flat, f32),
            pltpu.VMEM(coarse_factor.shape, f32),
            pltpu.VMEM(lane_tables.shape, bf16),
            pltpu.VMEM(row_tables.shape, bf16),
            pltpu.VMEM(flat, f32),
            pltpu.VMEM((2, 2, lay.slab, lanes), f32),
            pltpu.VMEM((2, 2, lay.slab, lanes), f32),
            pltpu.VMEM((2, 2, ex, n, lanes), f32),
            pltpu.VMEM((2, 2, ex, n, lanes), f32),
            pltpu.VMEM((2, 2, 2, n, lanes), f32),
            pltpu.VMEM((lay.lines * ey, lanes), f32),
            pltpu.VMEM(((2 + ex) * lay.slab, lanes), f32),
            pltpu.VMEM((lay.coarse_lines * 8, lanes), f32),
            pltpu.VMEM((lay.pack, lay.share, lanes), f32),
            pltpu.VMEM((lay.pack, lay.share, lanes), f32),
            pltpu.VMEM((lay.far, lay.share, lanes), f32),
            pltpu.VMEM((lay.pack, lay.share, lanes), f32),
            pltpu.VMEM((ex, ey, lanes), f32),
            pltpu.VMEM((8, ey, lanes), f32),
            pltpu.VMEM((8, ey, lanes), f32),
            pltpu.VMEM((2, lay.coarse_lines, ex, lanes), f32),
            pltpu.VMEM((2, lay.coarse_lines, ex, lanes), f32),
            pltpu.VMEM((2, 3, ey, lanes), f32),
            pltpu.VMEM((2, 3, ey, lanes), f32),
            pltpu.SemaphoreType.DMA((6, 4)),
            pltpu.SemaphoreType.DMA((2, 8)),
            pltpu.SemaphoreType.DMA((2, 8)),
            pltpu.SemaphoreType.DMA((8,)),
            pltpu.SemaphoreType.DMA((8,)),
            pltpu.SemaphoreType.DMA((2, 2)),
            pltpu.SemaphoreType.DMA((2, 2)),
            pltpu.SemaphoreType.DMA((3,)),
            pltpu.SemaphoreType.DMA((3,)),
        ]
        grid = (3, ex + 2, ey, lanes)
        residual, solved, grid_values = pl.pallas_call(
            functools.partial(step_kernel, lay, derivative, vectors),
            out_shape=[
                jax.ShapeDtypeStruct(flat, f32),
                jax.ShapeDtypeStruct(flat, f32),
                jax.ShapeDtypeStruct(grid, f32),
            ],
            in_specs=[hbm] * 9,
            out_specs=[vmem] * 3,
            scratch_shapes=scratch,
            compiler_params=pltpu.CompilerParams(
                collective_id=0, has_side_effects=True, vmem_limit_bytes=40 * 1024 * 1024
            ),
            name="adjoint_step",
        )(
            *[
                pltpu.with_memory_space_constraint(array, pltpu.HBM)
                for array in (
                    adjoint.reshape(flat),
                    right_side.reshape(flat),
                    velocity.reshape((3,) + flat),
                    conductivity.reshape(flat),
                    mass_term.reshape(flat),
                    fdm_inverse.reshape(flat),
                    coarse_factor,
                    jnp.asarray(lane_tables),
                    jnp.asarray(row_tables),
                )
            ]
        )
        residual, correction = pl.pallas_call(
            functools.partial(finish_kernel, lay),
            out_shape=[pltpu.HBM(flat, f32)] * 2,
            in_specs=[vmem] * 3,
            out_specs=[hbm] * 2,
            scratch_shapes=[
                pltpu.VMEM(flat, f32),
                pltpu.VMEM((ex, 3, lay.slab, lanes), f32),
                pltpu.SemaphoreType.DMA((1 + ex,)),
            ],
            name="finish",
        )(
            *[
                pltpu.with_memory_space_constraint(array, pltpu.VMEM)
                for array in (residual, solved, grid_values)
            ]
        )
        return residual.reshape(adjoint.shape), correction.reshape(adjoint.shape)

    field = P("grp", None, "dev", None, None)
    in_specs = (
        field,
        field,
        P(None, "grp", None, "dev", None, None),
        field,
        field,
        field,
        P(("grp", "dev"), None),
    )
    return jax.shard_map(
        body, mesh=mesh, in_specs=in_specs, out_specs=(field, field), check_vma=False
    )
```

```python
import functools
import math

import jax
import jax.numpy as jnp
import ml_dtypes
import numpy as np
from jax import lax
from jax.experimental import pallas as pl
from jax.experimental.pallas import tpu as pltpu
from jax.sharding import PartitionSpec as P

GLL_POINTS = [
    -1.0,
    -0.871740148509607,
    -0.591700181433142,
    -0.209299217902479,
    0.209299217902479,
    0.591700181433142,
    0.871740148509607,
    1.0,
]


def legendre_value(point, highest):
    previous = 1.0
    current = point
    for degree in range(1, highest):
        previous, current = (
            current,
            ((2 * degree + 1) * point * current - degree * previous) / (degree + 1),
        )
    return current


def identity_list(dimension):
    return [
        [1.0 if row_index == col_index else 0.0 for col_index in range(dimension)]
        for row_index in range(dimension)
    ]


def transpose_list(matrix):
    return [
        [matrix[row_index][col_index] for row_index in range(len(matrix))]
        for col_index in range(len(matrix[0]))
    ]


def matrix_product(left, right):
    inner_size = len(right)
    return [
        [
            sum((left[row_index][inner] * right[inner][col_index] for inner in range(inner_size)))
            for col_index in range(len(right[0]))
        ]
        for row_index in range(len(left))
    ]


def jacobi_eigen(matrix):
    current = [list(line) for line in matrix]
    dimension = len(matrix)
    rotations = identity_list(dimension)
    for repeat in range(12):
        for row_index in range(dimension - 1):
            for col_index in range(row_index + 1, dimension):
                angle = 0.5 * math.atan2(
                    2.0 * current[row_index][col_index],
                    current[row_index][row_index] - current[col_index][col_index],
                )
                cosine = math.cos(angle)
                sine_value = math.sin(angle)
                rotation = identity_list(dimension)
                rotation[row_index][row_index] = cosine
                rotation[col_index][col_index] = cosine
                rotation[row_index][col_index] = -sine_value
                rotation[col_index][row_index] = sine_value
                current = matrix_product(
                    matrix_product(transpose_list(rotation), current), rotation
                )
                rotations = matrix_product(rotations, rotation)
    ordering = sorted(range(dimension), key=lambda position: current[position][position])
    return [
        [rotations[row_index][position] for position in ordering] for row_index in range(dimension)
    ]


def element_tables():
    total_points = len(GLL_POINTS)
    weights_bary = []
    for row_index in range(total_points):
        product_value = 1.0
        for col_index in range(total_points):
            if col_index != row_index:
                product_value = product_value * (GLL_POINTS[row_index] - GLL_POINTS[col_index])
        weights_bary.append(1.0 / product_value)
    derivative = [[0.0] * total_points for row_index in range(total_points)]
    for row_index in range(total_points):
        for col_index in range(total_points):
            if col_index != row_index:
                derivative[row_index][col_index] = (
                    weights_bary[col_index]
                    / weights_bary[row_index]
                    / (GLL_POINTS[row_index] - GLL_POINTS[col_index])
                )
        derivative[row_index][row_index] = -sum(derivative[row_index])
    quadrature = [
        2.0 / ((total_points - 1) * total_points * legendre_value(point, total_points - 1) ** 2)
        for point in GLL_POINTS
    ]
    stiffness = [
        [
            sum(
                (
                    derivative[inner][row_index] * quadrature[inner] * derivative[inner][col_index]
                    for inner in range(total_points)
                )
            )
            + (quadrature[row_index] if row_index == col_index else 0.0)
            for col_index in range(total_points)
        ]
        for row_index in range(total_points)
    ]
    return (derivative, jacobi_eigen(stiffness))


def block_diagonal(blocks, matrix):
    node_count = len(matrix)
    total = blocks * node_count
    return [
        [
            (
                matrix[row_index % node_count][col_index % node_count]
                if row_index // node_count == col_index // node_count
                else 0.0
            )
            for col_index in range(total)
        ]
        for row_index in range(total)
    ]


def assembly_table(blocks, node_count):
    total = blocks * node_count
    shared_index = [
        position // node_count * (node_count - 1) + position % node_count
        for position in range(total)
    ]
    return [
        [
            1.0 if shared_index[row_index] == shared_index[col_index] else 0.0
            for col_index in range(total)
        ]
        for row_index in range(total)
    ]

MESH_IDS = pl.DeviceIdType.MESH
TILE = 128
PACK = 16


def split_halves(values):
    high = values.astype(jnp.bfloat16)
    return high, (values - high.astype(jnp.float32)).astype(jnp.bfloat16)


def lane_operator(table, field):
    high, low = split_halves(field)
    stacked = jnp.concatenate([table, table], axis=0)
    product = jnp.dot(
        jnp.concatenate([high, low], axis=1), stacked, preferred_element_type=jnp.float32
    )
    return product[:, :TILE] + product[:, TILE:]


def row_operator(table, field):
    high, low = split_halves(field)
    stacked = jnp.concatenate([table, table], axis=1)
    results = []
    for start in range(0, field.shape[0], 2 * TILE):
        first, second = slice(start, start + TILE), slice(start + TILE, start + 2 * TILE)
        operand = jnp.concatenate(
            [
                jnp.concatenate([high[first], low[first]], axis=0),
                jnp.concatenate([high[second], low[second]], axis=0),
            ],
            axis=1,
        )
        product = jnp.dot(stacked, operand, preferred_element_type=jnp.float32)
        summed = product[:TILE] + product[TILE:]
        results += [summed[:, :TILE], summed[:, TILE:]]
    return jnp.concatenate(results, axis=0)


def weighted(coefficients, terms):
    total = terms[0] * coefficients[0]
    for coefficient, term in zip(coefficients[1:], terms[1:]):
        total = total + term * coefficient
    return total


def mirrored(layers):
    count = len(layers)
    half = count // 2
    sums = [layers[k] + layers[count - 1 - k] for k in range(half)]
    gaps = [layers[k] - layers[count - 1 - k] for k in range(half)]
    return sums, gaps


def odd_operator(matrix, layers):
    count = len(layers)
    half = count // 2
    sums, gaps = mirrored(layers)
    lower, upper = [], []
    for row in range(half):
        line = matrix[row]
        even = weighted([0.5 * (line[k] + line[count - 1 - k]) for k in range(half)], sums)
        odd = weighted([0.5 * (line[k] - line[count - 1 - k]) for k in range(half)], gaps)
        lower.append(odd + even)
        upper.append(odd - even)
    return lower + upper[::-1]


def to_modes(vectors, layers):
    count = len(layers)
    half = count // 2
    sums, gaps = mirrored(layers)
    return [
        weighted([vectors[k][mode] for k in range(half)], gaps if mode % 2 else sums)
        for mode in range(count)
    ]


def from_modes(vectors, modes):
    count = len(modes)
    half = count // 2
    lower, upper = [], []
    for row in range(half):
        even = weighted(vectors[row][0::2], modes[0::2])
        odd = weighted(vectors[row][1::2], modes[1::2])
        lower.append(even + odd)
        upper.append(even - odd)
    return lower + upper[::-1]


def half_pair(matrix):
    table = np.asarray(matrix, np.float64).astype(np.float32)
    high = table.astype(ml_dtypes.bfloat16)
    low = (table - high.astype(np.float32)).astype(ml_dtypes.bfloat16)
    return high, low


def lane_table(matrix):
    return np.concatenate(half_pair(matrix), axis=1)


def row_table(matrix):
    return np.concatenate(half_pair(matrix), axis=0)


def operator_tables(nodes, lanes):
    derivative, vectors = element_tables()
    blocks = lanes // nodes
    backward_z = block_diagonal(blocks, derivative)
    vectors_z = block_diagonal(blocks, vectors)
    joined = assembly_table(blocks, nodes)
    physical_joined = (np.asarray(transpose_list(vectors_z)) @ np.asarray(joined)).tolist()
    lane_tables = np.stack(
        [
            lane_table(transpose_list(backward_z)),
            lane_table(backward_z),
            lane_table(vectors_z),
            lane_table(physical_joined),
        ]
    )
    row_tables = np.stack(
        [
            row_table(backward_z),
            row_table(transpose_list(backward_z)),
            row_table(transpose_list(vectors_z)),
            row_table(vectors_z),
        ]
    )
    return derivative, vectors, lane_tables, row_tables


class Layout:
    def __init__(self, elements_x, nodes, elements_y, lanes, groups, devices, coarse):
        self.ex, self.n, self.ey, self.lanes = elements_x, nodes, elements_y, lanes
        self.groups, self.devices = groups, devices
        self.slab = elements_y * nodes
        self.chunk = nodes * self.slab
        self.rows = elements_x * self.chunk
        self.lines = elements_x * nodes
        self.columns = elements_x * elements_y
        self.pack = math.gcd(PACK, devices)
        self.far = groups * (devices // self.pack)
        self.coarse = coarse
        self.coarse_lines = coarse // lanes
        self.share = self.coarse_lines // self.pack


def step_kernel(
    lay, derivative, vectors,
    adjoint, right_side, velocity, conductivity, mass_term, fdm_inverse, factor, lane_t, row_t,
    residual, correction, grid,
    v_adj, v_rs, v_vel, v_con, v_mass, v_fdm, v_fac, v_lane, v_row, flux_sum,
    local, side_send, side_recv, row_send, row_recv, edge_recv, halo_lines,
    column_sum, inner_part, near_src, near_in, far_in, full_in,
    sum_tile, note_send, note_recv, rim_send, rim_recv, ring_out, ring_in,
    load_sem, face_send, face_recv, note_sent, note_got, rim_sem, ring_sem, sum_send, sum_recv,
):
    ex, n, ey, lanes = lay.ex, lay.n, lay.ey, lay.lanes
    slab, chunk, lines, columns = lay.slab, lay.chunk, lay.lines, lay.columns
    group = lax.axis_index("grp")
    device = lax.axis_index("dev")
    near_id = lax.rem(device, lay.pack)
    block_id = device // lay.pack
    far_blocks = lay.devices // lay.pack
    far_id = group * far_blocks + block_id

    def near_device(index):
        return (group, block_id * lay.pack + index)

    def far_device(index):
        return (index // far_blocks, lax.rem(index, far_blocks) * lay.pack + near_id)

    def neighbour(step_g, step_d):
        return (
            lax.rem(group + step_g + lay.groups, lay.groups),
            lax.rem(device + step_d + lay.devices, lay.devices),
        )

    steps = [(g, d) for g in (-1, 0, 1) for d in (-1, 0, 1) if (g, d) != (0, 0)]

    def chunk_rows(x):
        return pl.ds(pl.multiple_of(x * chunk, chunk), chunk)

    def chunk_loads(x):
        rows = chunk_rows(x)
        return [
            pltpu.make_async_copy(adjoint.at[rows], v_adj.at[rows], load_sem.at[0, x]),
            pltpu.make_async_copy(conductivity.at[rows], v_con.at[rows], load_sem.at[1, x]),
            pltpu.make_async_copy(velocity.at[:, rows], v_vel.at[:, rows], load_sem.at[2, x]),
            pltpu.make_async_copy(mass_term.at[rows], v_mass.at[rows], load_sem.at[3, x]),
        ]

    def table_loads(part):
        half = pl.ds(2 * part, 2)
        return [
            pltpu.make_async_copy(lane_t.at[half], v_lane.at[half], load_sem.at[4 + part, 0]),
            pltpu.make_async_copy(row_t.at[half], v_row.at[half], load_sem.at[4 + part, 1]),
        ]

    late_loads = [
        pltpu.make_async_copy(right_side, v_rs, load_sem.at[4, 2]),
        pltpu.make_async_copy(factor, v_fac, load_sem.at[4, 3]),
        pltpu.make_async_copy(fdm_inverse, v_fdm, load_sem.at[5, 2]),
    ] + table_loads(1)
    for copy in chunk_loads(0) + table_loads(0):
        copy.start()

    def ring_steps(offset, size):
        return min(offset % size, -offset % size)

    def near_hops(offset):
        return ring_steps(offset // 2, 4) + offset // 8

    def far_hops(offset):
        return 2 * ring_steps(offset // far_blocks, lay.groups) + ring_steps(offset, far_blocks)

    barrier = pltpu.get_barrier_semaphore()
    for offset in sorted(range(1, lay.far), key=far_hops, reverse=True):
        target = far_device(lax.rem(far_id + offset, lay.far))
        pl.semaphore_signal(barrier, inc=1, device_id=target, device_id_type=MESH_IDS)


    lane_index = lax.broadcasted_iota(jnp.int32, (1, lanes), 1)
    lane_node = lax.rem(lane_index, n)
    is_upper = lane_node == n - 1
    shared = jnp.where(
        (is_upper & (lane_index != lanes - 1)) | ((lane_node == 0) & (lane_index != 0)), 1.0, 0.0
    ).astype(jnp.float32)
    line_index = lax.broadcasted_iota(jnp.int32, (n, lanes), 0)
    first_line = line_index == 0
    last_line = line_index == n - 1
    for step in steps:
        pl.semaphore_signal(barrier, inc=1, device_id=neighbour(*step), device_id_type=MESH_IDS)
    for offset in range(1, lay.pack):
        target = near_device(lax.rem(near_id + offset, lay.pack))
        pl.semaphore_signal(barrier, inc=1, device_id=target, device_id_type=MESH_IDS)
    for copy in chunk_loads(1):
        copy.start()

    def layers_of(field):
        return [field[k * slab : (k + 1) * slab] for k in range(n)]

    def load_chunk(x):
        for copy in chunk_loads(x) + (table_loads(0) if x == 0 else []):
            copy.wait()
        if x + 2 < ex:
            for copy in chunk_loads(x + 2):
                copy.start()
        elif x + 2 == ex:
            late_loads[0].start()
        else:
            for copy in late_loads[1:]:
                copy.start()

    copies_of = 1.0 + shared
    at_low = [line[0] for line in derivative]
    at_high = [line[n - 1] for line in derivative]
    third_weight = jnp.zeros((1, lanes), jnp.float32)
    for node in range(n):
        ends = jnp.where(lane_index >= n, at_low[node], 0.0)
        ends = ends + jnp.where(lane_index < lanes - n, at_high[node], 0.0)
        third_weight = third_weight + jnp.where(lane_node == node, ends, 0.0)

    def flux_chunk(x):
        rows = pl.ds(x * chunk, chunk)
        field = v_adj[rows]
        diffusion = v_con[rows]
        third = diffusion * lane_operator(v_lane[0], field) + v_vel[2, rows] * field
        second = diffusion * row_operator(v_row[0], field) + v_vel[1, rows] * field
        gradient = jnp.concatenate(odd_operator(derivative, layers_of(field)), axis=0)
        first = diffusion * gradient + v_vel[0, rows] * field
        mass = v_mass[rows] * field
        v_vel[0, rows] = first
        v_vel[1, rows] = second
        v_vel[2, rows] = third
        local[rows] = mass
        first, second, third, mass = [layers_of(value) for value in (first, second, third, mass)]

        def whole(layers):
            total = layers[0]
            for layer in layers[1:]:
                total = total + layer
            return total

        parts = [
            (whole(mass), whole(third), whole(second)),
            (mass[0] + weighted(at_low, first), third[0], second[0]),
            (mass[n - 1] + weighted(at_high, first), third[n - 1], second[n - 1]),
        ]
        for part, (plain, lanewise, linewise) in enumerate(parts):
            flux_sum[part, x, 0] = copies_of * plain + third_weight * lanewise
            flux_sum[part, x, 1] = copies_of * linewise

    def divergence(x):
        rows = pl.ds(x * chunk, chunk)
        total = lane_operator(v_lane[1], v_vel[2, rows]) + row_operator(v_row[1], v_vel[1, rows])
        total = total + jnp.concatenate(
            odd_operator(transpose_list(derivative), layers_of(v_vel[0, rows])), axis=0
        )
        total = total + local[rows]
        crossed = jnp.where(
            is_upper, pltpu.roll(total, lanes - 1, axis=1), pltpu.roll(total, 1, axis=1)
        )
        local[rows] = total + shared * crossed

    def joined_sum(slot):
        plain = [column_sum[pl.ds(slot * 2 * slab + j, ey, stride=n)] for j in range(n)]
        linewise = [column_sum[pl.ds((slot * 2 + 1) * slab + j, ey, stride=n)] for j in range(n)]
        total = plain[0]
        for value in plain[1:]:
            total = total + value
        lower = plain[0] + weighted(at_low, linewise)
        upper = plain[n - 1] + weighted(at_high, linewise)
        below = jnp.where(first_line, 0.0, pltpu.roll(upper, 1, axis=0))
        above = jnp.where(last_line, 0.0, pltpu.roll(lower, ey - 1, axis=0))
        return total + below + above, lower, upper

    for x in range(ex):
        load_chunk(x)
        flux_chunk(x)

    low_g = jnp.where(group > 0, 1.0, 0.0).astype(jnp.float32)
    high_g = jnp.where(group < lay.groups - 1, 1.0, 0.0).astype(jnp.float32)
    low_d = jnp.where(device > 0, 1.0, 0.0).astype(jnp.float32)
    high_d = jnp.where(device < lay.devices - 1, 1.0, 0.0).astype(jnp.float32)
    gates_g, gates_d = (low_g, high_g), (low_d, high_d)

    def face_copies(phase):
        copies = []
        for index, (g, d) in enumerate(steps):
            if d == 0:
                source, target = side_send.at[phase, (g + 1) // 2], side_recv.at[phase, (1 - g) // 2]
            elif g == 0:
                source, target = row_send.at[phase, (d + 1) // 2], row_recv.at[phase, (1 - d) // 2]
            else:
                x = 0 if g < 0 else ex - 1
                source = row_send.at[phase, (d + 1) // 2, x]
                target = edge_recv.at[phase, (1 - g) // 2, (1 - d) // 2]
            copies.append(
                pltpu.make_async_remote_copy(
                    src_ref=source,
                    dst_ref=target,
                    send_sem=face_send.at[phase, index],
                    recv_sem=face_recv.at[phase, index],
                    device_id=neighbour(g, d),
                    device_id_type=MESH_IDS,
                )
            )
        return copies

    def pack_faces(field, phase):
        side_send[phase, 0] = field[pl.ds(0, slab)]
        side_send[phase, 1] = field[pl.ds(lay.rows - slab, slab)]
        for x in range(ex - 1):
            upper, lower = pl.ds((x + 1) * chunk - slab, slab), pl.ds((x + 1) * chunk, slab)
            both = field[upper] + field[lower]
            field[upper] = both
            field[lower] = both
        for x in range(ex):
            row_send[phase, 0, x] = field[pl.ds(x * chunk, n, stride=slab)]
            row_send[phase, 1, x] = field[pl.ds(x * chunk + slab - 1, n, stride=slab)]

    def send_faces(phase):
        copies = face_copies(phase)
        for copy in copies:
            copy.start()
        return copies

    def join_faces(field, phase, copies):
        for copy in copies:
            copy.wait_recv()
        head, tail = pl.ds(0, slab), pl.ds(lay.rows - slab, slab)
        field[head] = field[head] + low_g * side_recv[phase, 0]
        field[tail] = field[tail] + high_g * side_recv[phase, 1]
        for d in range(2):
            low_edge = edge_recv[phase, 0, d, pl.ds(n - 1, n, stride=0)]
            high_edge = edge_recv[phase, 1, d, pl.ds(0, n, stride=0)]
            first = row_recv[phase, d, 0] + jnp.where(first_line, low_g * low_edge, 0.0)
            row_recv[phase, d, 0] = first
            last = row_recv[phase, d, ex - 1] + jnp.where(last_line, high_g * high_edge, 0.0)
            row_recv[phase, d, ex - 1] = last
            spot = 0 if d == 0 else n - 1
            for x in range(ex):
                halo_lines[pl.ds(x * slab + spot, n, stride=n)] = gates_d[d] * row_recv[phase, d, x]
        starts = pl.ds(0, lines * ey, stride=n)
        ends = pl.ds(n - 1, lines * ey, stride=n)
        lower = field[starts].reshape(lines, ey, lanes)
        upper = field[ends].reshape(lines, ey, lanes)
        outside = halo_lines[...].reshape(lines, ey, lanes)
        from_below = jnp.where(first_line, outside, pltpu.roll(upper, 1, axis=1))
        from_above = jnp.where(last_line, outside, pltpu.roll(lower, ey - 1, axis=1))
        field[starts] = (lower + from_below).reshape(lines * ey, lanes)
        field[ends] = (upper + from_above).reshape(lines * ey, lanes)

    for part in range(2):
        column_sum[pl.ds(part * slab, slab)] = flux_sum[1, 0, part]
        column_sum[pl.ds((2 + part) * slab, slab)] = flux_sum[2, ex - 1, part]
        for x in range(ex):
            total = flux_sum[0, x, part]
            if x > 0:
                total = total + flux_sum[2, x - 1, part]
            if x < ex - 1:
                total = total + flux_sum[1, x + 1, part]
            column_sum[pl.ds((4 + 2 * x + part) * slab, slab)] = total
    for side in range(2):
        total, lower, upper = joined_sum(side)
        note_send[side] = total
        note_send[4 + 2 * side] = jnp.broadcast_to(lower[0:1], (ey, lanes))
        note_send[5 + 2 * side] = jnp.broadcast_to(upper[ey - 1 : ey], (ey, lanes))
    for x in range(ex):
        total, lower, upper = joined_sum(2 + x)
        sum_tile[x] = total
        note_send[2, pl.ds(x, 1)] = lower[0:1]
        note_send[3, pl.ds(x, 1)] = upper[ey - 1 : ey]

    def exists(g, d):
        found = (group + g >= 0) & (group + g < lay.groups)
        return found & (device + d >= 0) & (device + d < lay.devices)

    def start_inside(copies, ways):
        for copy, (g, d) in zip(copies, ways):
            pl.when(exists(g, d))(copy.start)

    def await_inside(copies, ways):
        for copy, (g, d) in zip(copies, ways):
            pl.when(exists(-g, -d))(copy.wait_recv)

    def await_sent(copies, ways):
        for copy, (g, d) in zip(copies, ways):
            pl.when(exists(g, d))(copy.wait_send)

    whole_line = jnp.zeros((n, lanes), jnp.int32)
    has_low_g, has_high_g = whole_line + group > 0, whole_line + group < lay.groups - 1
    has_low_d, has_high_d = whole_line + device > 0, whole_line + device < lay.devices - 1

    def note_slot(g, d):
        if d == 0:
            return (g + 1) // 2
        if g == 0:
            return 2 + (d + 1) // 2
        return 4 + 2 * ((g + 1) // 2) + (d + 1) // 2

    note_copies = [
        pltpu.make_async_remote_copy(
            src_ref=note_send.at[note_slot(g, d)],
            dst_ref=note_recv.at[note_slot(-g, -d)],
            send_sem=note_sent.at[index],
            recv_sem=note_got.at[index],
            device_id=neighbour(g, d),
            device_id_type=MESH_IDS,
        )
        for index, (g, d) in enumerate(steps)
    ]

    pl.semaphore_wait(barrier, len(steps) + lay.pack - 1 + lay.far - 1)
    start_inside(note_copies, steps)
    late_loads[0].wait()
    for x in range(ex):
        layers = layers_of(v_rs[pl.ds(x * chunk, chunk)])
        total = layers[0]
        for layer in layers[1:]:
            total = total + layer
        column_sum[pl.ds(x * slab, slab)] = total
    for x in range(ex):
        total = column_sum[pl.ds(x * slab, ey, stride=n)]
        for j in range(1, n):
            total = total + column_sum[pl.ds(x * slab + j, ey, stride=n)]
        sum_tile[x] = total - sum_tile[x]
    late_loads[1].wait()
    def rim_block(line, carry):
        spot = pl.ds(pl.multiple_of(line * lanes, lanes), lanes)
        for x in range(ex):
            rim_send[0, line, pl.ds(x, 1)] = v_fac[pl.ds(x * ey, 1), spot]
            rim_send[1, line, pl.ds(x, 1)] = v_fac[pl.ds(x * ey + ey - 1, 1), spot]
        return carry

    lax.fori_loop(0, lay.coarse_lines, rim_block, 0)

    rim_copies = [
        pltpu.make_async_remote_copy(
            src_ref=rim_send.at[(d + 1) // 2],
            dst_ref=rim_recv.at[(1 - d) // 2],
            send_sem=rim_sem.at[0, (d + 1) // 2],
            recv_sem=rim_sem.at[1, (d + 1) // 2],
            device_id=neighbour(0, d),
            device_id_type=MESH_IDS,
        )
        for d in (-1, 1)
    ]
    for copy in rim_copies:
        copy.start()
    for x in range(ex):
        divergence(x)
    pack_faces(local, 0)
    first_copies = send_faces(0)
    await_inside(note_copies, steps)
    sums = []
    for x in range(ex):
        total = sum_tile[x]
        ends = []
        for d in range(2):
            end = note_recv[2 + d, pl.ds(x, ey, stride=0)]
            if x == 0:
                end = end + jnp.where(has_low_g, note_recv[4 + d], 0.0)
            if x == ex - 1:
                end = end + jnp.where(has_high_g, note_recv[6 + d], 0.0)
            ends.append(jnp.where((has_low_d, has_high_d)[d], end, 0.0))
        if x == 0:
            total = total - jnp.where(has_low_g, note_recv[0], 0.0)
        if x == ex - 1:
            total = total - jnp.where(has_high_g, note_recv[1], 0.0)
        total = total - jnp.where(first_line, ends[0], 0.0) - jnp.where(last_line, ends[1], 0.0)
        sums.append(total)
    means = jnp.sum(jnp.concatenate(sums, axis=0), axis=1, keepdims=True)
    means = jnp.broadcast_to(means * (1.0 / float(n * n * lanes)), (columns, lanes))

    def inner_block(block, carry):
        for k in range(8):
            line = block * 8 + k
            piece = v_fac[:, pl.ds(pl.multiple_of(line * lanes, lanes), lanes)] * means
            total = piece[0:8]
            for start in range(8, columns, 8):
                total = total + piece[start : start + 8]
            inner_part[pl.ds(pl.multiple_of(line * 8, 8), 8)] = total
        return carry

    lax.fori_loop(0, lay.coarse_lines // 8, inner_block, 0)
    for index in range(lay.pack):
        base = index * lay.share * 8
        total = inner_part[pl.ds(base, lay.share, stride=8)]
        for k in range(1, 8):
            total = total + inner_part[pl.ds(base + k, lay.share, stride=8)]
        near_src[index] = total

    def exchange(stage, count, own, device_of, source_of, buffer):
        def send(offset, carry):
            index = lax.rem(own + offset, count)
            pltpu.make_async_remote_copy(
                src_ref=source_of(index),
                dst_ref=buffer.at[own],
                send_sem=sum_send.at[stage],
                recv_sem=sum_recv.at[stage],
                device_id=device_of(index),
                device_id_type=MESH_IDS,
            ).start()
            return carry

        for offset in sorted(range(1, count), key=far_hops if stage == 1 else near_hops, reverse=True):
            send(offset, 0)

    def await_exchange(stage, count, buffer, sem):
        part = buffer.at[pl.ds(0, count - 1)]
        pltpu.make_async_copy(part, part, sem.at[stage]).wait()

    exchange(0, lay.pack, near_id, near_device, lambda index: near_src.at[index], near_in)
    near_in[near_id] = near_src[near_id]


    await_exchange(0, lay.pack, near_in, sum_recv)
    far_in[far_id] = jnp.sum(near_in[...], axis=0)
    exchange(1, lay.far, far_id, far_device, lambda index: far_in.at[far_id], far_in)

    join_faces(local, 0, first_copies)
    for x in range(ex):
        rows = pl.ds(x * chunk, chunk)
        residual[rows] = v_rs[rows] - local[rows]

    for copy in late_loads[2:]:
        copy.wait()

    def solve_chunk(x):
        rows = pl.ds(x * chunk, chunk)
        field = jnp.concatenate(to_modes(vectors, layers_of(residual[rows])), axis=0)
        field = row_operator(v_row[2], field)
        field = lane_operator(v_lane[2], field) * v_fdm[rows]
        field = lane_operator(v_lane[3], field)
        field = row_operator(v_row[3], field)
        correction[rows] = jnp.concatenate(from_modes(vectors, layers_of(field)), axis=0)

    for x in range(ex):
        solve_chunk(x)
    pack_faces(correction, 1)
    second_copies = send_faces(1)

    await_exchange(1, lay.far, far_in, sum_recv)
    full_in[near_id] = jnp.sum(far_in[...], axis=0)
    exchange(2, lay.pack, near_id, near_device, lambda index: full_in.at[near_id], full_in)

    for copy in rim_copies:
        copy.wait_recv()

    await_exchange(2, lay.pack, full_in, sum_recv)

    def value_block(index, totals):
        inside, left, right = totals
        for k in range(lay.share):
            line = index * lay.share + k
            value = jnp.broadcast_to(full_in[index, pl.ds(k, 1)], (columns, lanes))
            spot = pl.ds(pl.multiple_of(line * lanes, lanes), lanes)
            inside = inside + v_fac[:, spot] * value
            left = left + rim_recv[0, line] * value[:ex]
            right = right + rim_recv[1, line] * value[:ex]
        return inside, left, right

    none = jnp.zeros((ex, lanes), jnp.float32)
    inside, left, right = lax.fori_loop(
        0, lay.pack, value_block, (jnp.zeros((columns, lanes), jnp.float32), none, none)
    )
    inside = jnp.broadcast_to(jnp.sum(inside, axis=1, keepdims=True), (columns, lanes))
    left = low_d * jnp.sum(left, axis=1, keepdims=True)
    right = high_d * jnp.sum(right, axis=1, keepdims=True)
    for x in range(ex):
        grid[0, 1 + x] = inside[x * ey : (x + 1) * ey]
        grid[1, 1 + x] = jnp.broadcast_to(left[x : x + 1], (ey, lanes))
        grid[2, 1 + x] = jnp.broadcast_to(right[x : x + 1], (ey, lanes))
    for part in range(3):
        ring_out[0, part] = grid[part, 1]
        ring_out[1, part] = grid[part, ex]
    ring_copies = [
        pltpu.make_async_remote_copy(
            src_ref=ring_out.at[(g + 1) // 2],
            dst_ref=ring_in.at[(1 - g) // 2],
            send_sem=ring_sem.at[0, (g + 1) // 2],
            recv_sem=ring_sem.at[1, (g + 1) // 2],
            device_id=neighbour(g, 0),
            device_id_type=MESH_IDS,
        )
        for g in (-1, 1)
    ]
    ring_ways = [(-1, 0), (1, 0)]
    start_inside(ring_copies, ring_ways)
    join_faces(correction, 1, second_copies)
    await_inside(ring_copies, ring_ways)
    for part in range(3):
        grid[part, 0] = jnp.where(has_low_g, ring_in[0, part], 0.0)
        grid[part, ex + 1] = jnp.where(has_high_g, ring_in[1, part], 0.0)

    await_sent(note_copies, steps)
    await_sent(ring_copies, ring_ways)
    for copy in first_copies + rim_copies + second_copies:
        copy.wait_send()
    await_exchange(0, lay.pack, near_in, sum_send)
    await_exchange(1, lay.far, far_in, sum_send)
    await_exchange(2, lay.pack, full_in, sum_send)


def finish_kernel(lay, residual, solved, grid, out_residual, out_correction, staged, tile, sem):
    ex, n, ey, lanes, slab, chunk = lay.ex, lay.n, lay.ey, lay.lanes, lay.slab, lay.chunk
    copies = [pltpu.make_async_copy(residual, out_residual, sem.at[0])]
    copies[0].start()
    lane_index = lax.broadcasted_iota(jnp.int32, (1, lanes), 1)
    lane_node = lax.rem(lane_index, n)
    shared = ((lane_node == n - 1) & (lane_index != lanes - 1)) | (
        (lane_node == 0) & (lane_index != 0)
    )
    copies_of = jnp.where(shared, 2.0, 1.0).astype(jnp.float32)
    line_index = lax.broadcasted_iota(jnp.int32, (ey, lanes), 0)
    first_line, last_line = line_index == 0, line_index == ey - 1
    for x in range(ex):
        for part in range(3):
            sides = []
            for side in range(3):
                value = grid[side, x + 1]
                if part == 0:
                    value = value + grid[side, x]
                elif part == 2:
                    value = value + grid[side, x + 2]
                sides.append(value * copies_of)
            inside, left, right = sides
            below = jnp.where(first_line, left, pltpu.roll(inside, 1, axis=0))
            above = jnp.where(last_line, right, pltpu.roll(inside, ey - 1, axis=0))
            for j in range(n):
                value = inside
                if j == 0:
                    value = inside + below
                elif j == n - 1:
                    value = inside + above
                tile[x, part, pl.ds(j, ey, stride=n)] = value
        for layer in range(n):
            part = 0 if layer == 0 else 2 if layer == n - 1 else 1
            spot = pl.ds(x * chunk + layer * slab, slab)
            staged[spot] = solved[spot] + tile[x, part]
        rows = pl.ds(x * chunk, chunk)
        copy = pltpu.make_async_copy(staged.at[rows], out_correction.at[rows], sem.at[1 + x])
        copy.start()
        copies.append(copy)
    for copy in copies:
        copy.wait()


def solution(mesh):
    groups, devices = mesh.shape["grp"], mesh.shape["dev"]

    def body(adjoint, right_side, velocity, conductivity, mass_term, fdm_inverse, coarse_factor):
        ex, n, ey, _, lanes = adjoint.shape
        lay = Layout(ex, n, ey, lanes, groups, devices, coarse_factor.shape[1])
        derivative, vectors, lane_tables, row_tables = operator_tables(n, lanes)
        flat = (lay.rows, lanes)
        f32, bf16 = jnp.float32, jnp.bfloat16
        hbm = pl.BlockSpec(memory_space=pltpu.HBM)
        vmem = pl.BlockSpec(memory_space=pltpu.VMEM)
        scratch = [
            pltpu.VMEM(flat, f32),
            pltpu.VMEM(flat, f32),
            pltpu.VMEM((3,) + flat, f32),
            pltpu.VMEM(flat, f32),
            pltpu.VMEM(flat, f32),
            pltpu.VMEM(flat, f32),
            pltpu.VMEM(coarse_factor.shape, f32),
            pltpu.VMEM(lane_tables.shape, bf16),
            pltpu.VMEM(row_tables.shape, bf16),
            pltpu.VMEM((3, ex, 2, lay.slab, lanes), f32),
            pltpu.VMEM(flat, f32),
            pltpu.VMEM((2, 2, lay.slab, lanes), f32),
            pltpu.VMEM((2, 2, lay.slab, lanes), f32),
            pltpu.VMEM((2, 2, ex, n, lanes), f32),
            pltpu.VMEM((2, 2, ex, n, lanes), f32),
            pltpu.VMEM((2, 2, 2, n, lanes), f32),
            pltpu.VMEM((lay.lines * ey, lanes), f32),
            pltpu.VMEM((2 * (2 + ex) * lay.slab, lanes), f32),
            pltpu.VMEM((lay.coarse_lines * 8, lanes), f32),
            pltpu.VMEM((lay.pack, lay.share, lanes), f32),
            pltpu.VMEM((lay.pack, lay.share, lanes), f32),
            pltpu.VMEM((lay.far, lay.share, lanes), f32),
            pltpu.VMEM((lay.pack, lay.share, lanes), f32),
            pltpu.VMEM((ex, ey, lanes), f32),
            pltpu.VMEM((8, ey, lanes), f32),
            pltpu.VMEM((8, ey, lanes), f32),
            pltpu.VMEM((2, lay.coarse_lines, ex, lanes), f32),
            pltpu.VMEM((2, lay.coarse_lines, ex, lanes), f32),
            pltpu.VMEM((2, 3, ey, lanes), f32),
            pltpu.VMEM((2, 3, ey, lanes), f32),
            pltpu.SemaphoreType.DMA((6, 4)),
            pltpu.SemaphoreType.DMA((2, 8)),
            pltpu.SemaphoreType.DMA((2, 8)),
            pltpu.SemaphoreType.DMA((8,)),
            pltpu.SemaphoreType.DMA((8,)),
            pltpu.SemaphoreType.DMA((2, 2)),
            pltpu.SemaphoreType.DMA((2, 2)),
            pltpu.SemaphoreType.DMA((3,)),
            pltpu.SemaphoreType.DMA((3,)),
        ]
        grid = (3, ex + 2, ey, lanes)
        residual, solved, grid_values = pl.pallas_call(
            functools.partial(step_kernel, lay, derivative, vectors),
            out_shape=[
                jax.ShapeDtypeStruct(flat, f32),
                jax.ShapeDtypeStruct(flat, f32),
                jax.ShapeDtypeStruct(grid, f32),
            ],
            in_specs=[hbm] * 9,
            out_specs=[vmem] * 3,
            scratch_shapes=scratch,
            compiler_params=pltpu.CompilerParams(
                collective_id=0, has_side_effects=True, vmem_limit_bytes=40 * 1024 * 1024
            ),
            name="adjoint_step",
        )(
            *[
                pltpu.with_memory_space_constraint(array, pltpu.HBM)
                for array in (
                    adjoint.reshape(flat),
                    right_side.reshape(flat),
                    velocity.reshape((3,) + flat),
                    conductivity.reshape(flat),
                    mass_term.reshape(flat),
                    fdm_inverse.reshape(flat),
                    coarse_factor,
                    jnp.asarray(lane_tables),
                    jnp.asarray(row_tables),
                )
            ]
        )
        residual, correction = pl.pallas_call(
            functools.partial(finish_kernel, lay),
            out_shape=[pltpu.HBM(flat, f32)] * 2,
            in_specs=[vmem] * 3,
            out_specs=[hbm] * 2,
            scratch_shapes=[
                pltpu.VMEM(flat, f32),
                pltpu.VMEM((ex, 3, lay.slab, lanes), f32),
                pltpu.SemaphoreType.DMA((1 + ex,)),
            ],
            name="finish",
        )(
            *[
                pltpu.with_memory_space_constraint(array, pltpu.VMEM)
                for array in (residual, solved, grid_values)
            ]
        )
        return residual.reshape(adjoint.shape), correction.reshape(adjoint.shape)

    field = P("grp", None, "dev", None, None)
    in_specs = (
        field,
        field,
        P(None, "grp", None, "dev", None, None),
        field,
        field,
        field,
        P(("grp", "dev"), None),
    )
    return jax.shard_map(
        body, mesh=mesh, in_specs=in_specs, out_specs=(field, field), check_vma=False
    )
```

```python
import functools
import math

import jax
import jax.numpy as jnp
import ml_dtypes
import numpy as np
from jax import lax
from jax.experimental import pallas as pl
from jax.experimental.pallas import tpu as pltpu
from jax.sharding import PartitionSpec as P

GLL_POINTS = [
    -1.0,
    -0.871740148509607,
    -0.591700181433142,
    -0.209299217902479,
    0.209299217902479,
    0.591700181433142,
    0.871740148509607,
    1.0,
]


def legendre_value(point, highest):
    previous = 1.0
    current = point
    for degree in range(1, highest):
        previous, current = (
            current,
            ((2 * degree + 1) * point * current - degree * previous) / (degree + 1),
        )
    return current


def identity_list(dimension):
    return [
        [1.0 if row_index == col_index else 0.0 for col_index in range(dimension)]
        for row_index in range(dimension)
    ]


def transpose_list(matrix):
    return [
        [matrix[row_index][col_index] for row_index in range(len(matrix))]
        for col_index in range(len(matrix[0]))
    ]


def matrix_product(left, right):
    inner_size = len(right)
    return [
        [
            sum((left[row_index][inner] * right[inner][col_index] for inner in range(inner_size)))
            for col_index in range(len(right[0]))
        ]
        for row_index in range(len(left))
    ]


def jacobi_eigen(matrix):
    current = [list(line) for line in matrix]
    dimension = len(matrix)
    rotations = identity_list(dimension)
    for repeat in range(12):
        for row_index in range(dimension - 1):
            for col_index in range(row_index + 1, dimension):
                angle = 0.5 * math.atan2(
                    2.0 * current[row_index][col_index],
                    current[row_index][row_index] - current[col_index][col_index],
                )
                cosine = math.cos(angle)
                sine_value = math.sin(angle)
                rotation = identity_list(dimension)
                rotation[row_index][row_index] = cosine
                rotation[col_index][col_index] = cosine
                rotation[row_index][col_index] = -sine_value
                rotation[col_index][row_index] = sine_value
                current = matrix_product(
                    matrix_product(transpose_list(rotation), current), rotation
                )
                rotations = matrix_product(rotations, rotation)
    ordering = sorted(range(dimension), key=lambda position: current[position][position])
    return [
        [rotations[row_index][position] for position in ordering] for row_index in range(dimension)
    ]


def element_tables():
    total_points = len(GLL_POINTS)
    weights_bary = []
    for row_index in range(total_points):
        product_value = 1.0
        for col_index in range(total_points):
            if col_index != row_index:
                product_value = product_value * (GLL_POINTS[row_index] - GLL_POINTS[col_index])
        weights_bary.append(1.0 / product_value)
    derivative = [[0.0] * total_points for row_index in range(total_points)]
    for row_index in range(total_points):
        for col_index in range(total_points):
            if col_index != row_index:
                derivative[row_index][col_index] = (
                    weights_bary[col_index]
                    / weights_bary[row_index]
                    / (GLL_POINTS[row_index] - GLL_POINTS[col_index])
                )
        derivative[row_index][row_index] = -sum(derivative[row_index])
    quadrature = [
        2.0 / ((total_points - 1) * total_points * legendre_value(point, total_points - 1) ** 2)
        for point in GLL_POINTS
    ]
    stiffness = [
        [
            sum(
                (
                    derivative[inner][row_index] * quadrature[inner] * derivative[inner][col_index]
                    for inner in range(total_points)
                )
            )
            + (quadrature[row_index] if row_index == col_index else 0.0)
            for col_index in range(total_points)
        ]
        for row_index in range(total_points)
    ]
    return (derivative, jacobi_eigen(stiffness))


def block_diagonal(blocks, matrix):
    node_count = len(matrix)
    total = blocks * node_count
    return [
        [
            (
                matrix[row_index % node_count][col_index % node_count]
                if row_index // node_count == col_index // node_count
                else 0.0
            )
            for col_index in range(total)
        ]
        for row_index in range(total)
    ]


def assembly_table(blocks, node_count):
    total = blocks * node_count
    shared_index = [
        position // node_count * (node_count - 1) + position % node_count
        for position in range(total)
    ]
    return [
        [
            1.0 if shared_index[row_index] == shared_index[col_index] else 0.0
            for col_index in range(total)
        ]
        for row_index in range(total)
    ]

MESH_IDS = pl.DeviceIdType.MESH
TILE = 128
PACK = 16


def split_halves(values):
    high = values.astype(jnp.bfloat16)
    return high, (values - high.astype(jnp.float32)).astype(jnp.bfloat16)


def lane_operator(table, field):
    high, low = split_halves(field)
    stacked = jnp.concatenate([table, table], axis=0)
    product = jnp.dot(
        jnp.concatenate([high, low], axis=1), stacked, preferred_element_type=jnp.float32
    )
    return product[:, :TILE] + product[:, TILE:]


def row_operator(table, field):
    high, low = split_halves(field)
    stacked = jnp.concatenate([table, table], axis=1)
    results = []
    for start in range(0, field.shape[0], 2 * TILE):
        first, second = slice(start, start + TILE), slice(start + TILE, start + 2 * TILE)
        operand = jnp.concatenate(
            [
                jnp.concatenate([high[first], low[first]], axis=0),
                jnp.concatenate([high[second], low[second]], axis=0),
            ],
            axis=1,
        )
        product = jnp.dot(stacked, operand, preferred_element_type=jnp.float32)
        summed = product[:TILE] + product[TILE:]
        results += [summed[:, :TILE], summed[:, TILE:]]
    return jnp.concatenate(results, axis=0)


def weighted(coefficients, terms):
    total = terms[0] * coefficients[0]
    for coefficient, term in zip(coefficients[1:], terms[1:]):
        total = total + term * coefficient
    return total


def mirrored(layers):
    count = len(layers)
    half = count // 2
    sums = [layers[k] + layers[count - 1 - k] for k in range(half)]
    gaps = [layers[k] - layers[count - 1 - k] for k in range(half)]
    return sums, gaps


def odd_operator(matrix, layers):
    count = len(layers)
    half = count // 2
    sums, gaps = mirrored(layers)
    lower, upper = [], []
    for row in range(half):
        line = matrix[row]
        even = weighted([0.5 * (line[k] + line[count - 1 - k]) for k in range(half)], sums)
        odd = weighted([0.5 * (line[k] - line[count - 1 - k]) for k in range(half)], gaps)
        lower.append(odd + even)
        upper.append(odd - even)
    return lower + upper[::-1]


def to_modes(vectors, layers):
    count = len(layers)
    half = count // 2
    sums, gaps = mirrored(layers)
    return [
        weighted([vectors[k][mode] for k in range(half)], gaps if mode % 2 else sums)
        for mode in range(count)
    ]


def from_modes(vectors, modes):
    count = len(modes)
    half = count // 2
    lower, upper = [], []
    for row in range(half):
        even = weighted(vectors[row][0::2], modes[0::2])
        odd = weighted(vectors[row][1::2], modes[1::2])
        lower.append(even + odd)
        upper.append(even - odd)
    return lower + upper[::-1]


def half_pair(matrix):
    table = np.asarray(matrix, np.float64).astype(np.float32)
    high = table.astype(ml_dtypes.bfloat16)
    low = (table - high.astype(np.float32)).astype(ml_dtypes.bfloat16)
    return high, low


def lane_table(matrix):
    return np.concatenate(half_pair(matrix), axis=1)


def row_table(matrix):
    return np.concatenate(half_pair(matrix), axis=0)


def operator_tables(nodes, lanes):
    derivative, vectors = element_tables()
    blocks = lanes // nodes
    backward_z = block_diagonal(blocks, derivative)
    vectors_z = block_diagonal(blocks, vectors)
    joined = assembly_table(blocks, nodes)
    physical_joined = (np.asarray(transpose_list(vectors_z)) @ np.asarray(joined)).tolist()
    lane_tables = np.stack(
        [
            lane_table(transpose_list(backward_z)),
            lane_table(backward_z),
            lane_table(vectors_z),
            lane_table(physical_joined),
        ]
    )
    row_tables = np.stack(
        [
            row_table(backward_z),
            row_table(transpose_list(backward_z)),
            row_table(transpose_list(vectors_z)),
            row_table(vectors_z),
        ]
    )
    return derivative, vectors, lane_tables, row_tables


class Layout:
    def __init__(self, elements_x, nodes, elements_y, lanes, groups, devices, coarse):
        self.ex, self.n, self.ey, self.lanes = elements_x, nodes, elements_y, lanes
        self.groups, self.devices = groups, devices
        self.slab = elements_y * nodes
        self.chunk = nodes * self.slab
        self.rows = elements_x * self.chunk
        self.lines = elements_x * nodes
        self.columns = elements_x * elements_y
        self.pack = math.gcd(PACK, devices)
        self.far = groups * (devices // self.pack)
        self.coarse = coarse
        self.coarse_lines = coarse // lanes
        self.share = self.coarse_lines // self.pack


def step_kernel(
    lay, derivative, vectors,
    adjoint, right_side, velocity, conductivity, mass_term, fdm_inverse, factor, lane_t, row_t,
    residual, correction, grid,
    v_adj, v_rs, v_vel, v_con, v_mass, v_fdm, v_fac, v_lane, v_row, flux_sum,
    local, side_send, side_recv, row_send, row_recv, edge_recv, halo_lines,
    column_sum, inner_part, near_src, near_in, far_in, full_in,
    sum_tile, note_send, note_recv, rim_send, rim_recv, ring_out, ring_in,
    load_sem, face_send, face_recv, note_sent, note_got, rim_sem, ring_sem, sum_send, sum_recv,
):
    ex, n, ey, lanes = lay.ex, lay.n, lay.ey, lay.lanes
    slab, chunk, lines, columns = lay.slab, lay.chunk, lay.lines, lay.columns
    group = lax.axis_index("grp")
    device = lax.axis_index("dev")
    near_id = lax.rem(device, lay.pack)
    block_id = device // lay.pack
    far_blocks = lay.devices // lay.pack
    far_id = group * far_blocks + block_id

    def near_device(index):
        return (group, block_id * lay.pack + index)

    def far_device(index):
        return (index // far_blocks, lax.rem(index, far_blocks) * lay.pack + near_id)

    def neighbour(step_g, step_d):
        return (
            lax.rem(group + step_g + lay.groups, lay.groups),
            lax.rem(device + step_d + lay.devices, lay.devices),
        )

    steps = [(g, d) for g in (-1, 0, 1) for d in (-1, 0, 1) if (g, d) != (0, 0)]

    def chunk_rows(x):
        return pl.ds(pl.multiple_of(x * chunk, chunk), chunk)

    def chunk_loads(x):
        rows = chunk_rows(x)
        return [
            pltpu.make_async_copy(adjoint.at[rows], v_adj.at[rows], load_sem.at[0, x]),
            pltpu.make_async_copy(conductivity.at[rows], v_con.at[rows], load_sem.at[1, x]),
            pltpu.make_async_copy(velocity.at[:, rows], v_vel.at[:, rows], load_sem.at[2, x]),
            pltpu.make_async_copy(mass_term.at[rows], v_mass.at[rows], load_sem.at[3, x]),
        ]

    def table_loads(part):
        half = pl.ds(2 * part, 2)
        return [
            pltpu.make_async_copy(lane_t.at[half], v_lane.at[half], load_sem.at[4 + part, 0]),
            pltpu.make_async_copy(row_t.at[half], v_row.at[half], load_sem.at[4 + part, 1]),
        ]

    late_loads = [
        pltpu.make_async_copy(right_side, v_rs, load_sem.at[4, 2]),
        pltpu.make_async_copy(factor, v_fac, load_sem.at[4, 3]),
        pltpu.make_async_copy(fdm_inverse, v_fdm, load_sem.at[5, 2]),
    ] + table_loads(1)
    for copy in chunk_loads(0) + table_loads(0):
        copy.start()

    def ring_steps(offset, size):
        return min(offset % size, -offset % size)

    def near_hops(offset):
        return ring_steps(offset // 2, 4) + offset // 8

    def far_hops(offset):
        return 2 * ring_steps(offset // far_blocks, lay.groups) + ring_steps(offset, far_blocks)

    barrier = pltpu.get_barrier_semaphore()
    for offset in sorted(range(1, lay.far), key=far_hops, reverse=True):
        target = far_device(lax.rem(far_id + offset, lay.far))
        pl.semaphore_signal(barrier, inc=1, device_id=target, device_id_type=MESH_IDS)


    lane_index = lax.broadcasted_iota(jnp.int32, (1, lanes), 1)
    lane_node = lax.rem(lane_index, n)
    is_upper = lane_node == n - 1
    shared = jnp.where(
        (is_upper & (lane_index != lanes - 1)) | ((lane_node == 0) & (lane_index != 0)), 1.0, 0.0
    ).astype(jnp.float32)
    line_index = lax.broadcasted_iota(jnp.int32, (n, lanes), 0)
    first_line = line_index == 0
    last_line = line_index == n - 1
    for step in steps:
        pl.semaphore_signal(barrier, inc=1, device_id=neighbour(*step), device_id_type=MESH_IDS)
    for offset in range(1, lay.pack):
        target = near_device(lax.rem(near_id + offset, lay.pack))
        pl.semaphore_signal(barrier, inc=1, device_id=target, device_id_type=MESH_IDS)
    for copy in chunk_loads(1):
        copy.start()

    def layers_of(field):
        return [field[k * slab : (k + 1) * slab] for k in range(n)]

    def load_chunk(x):
        for copy in chunk_loads(x) + (table_loads(0) if x == 0 else []):
            copy.wait()
        if x + 2 < ex:
            for copy in chunk_loads(x + 2):
                copy.start()
        elif x + 2 == ex:
            late_loads[0].start()
        else:
            for copy in late_loads[1:]:
                copy.start()

    copies_of = 1.0 + shared
    at_low = [line[0] for line in derivative]
    at_high = [line[n - 1] for line in derivative]
    third_weight = jnp.zeros((1, lanes), jnp.float32)
    for node in range(n):
        ends = jnp.where(lane_index >= n, at_low[node], 0.0)
        ends = ends + jnp.where(lane_index < lanes - n, at_high[node], 0.0)
        third_weight = third_weight + jnp.where(lane_node == node, ends, 0.0)

    def flux_chunk(x):
        rows = pl.ds(x * chunk, chunk)
        field = v_adj[rows]
        diffusion = v_con[rows]
        third = diffusion * lane_operator(v_lane[0], field) + v_vel[2, rows] * field
        second = diffusion * row_operator(v_row[0], field) + v_vel[1, rows] * field
        gradient = jnp.concatenate(odd_operator(derivative, layers_of(field)), axis=0)
        first = diffusion * gradient + v_vel[0, rows] * field
        mass = v_mass[rows] * field
        v_vel[0, rows] = first
        v_vel[1, rows] = second
        v_vel[2, rows] = third
        local[rows] = mass
        first, second, third, mass = [layers_of(value) for value in (first, second, third, mass)]

        def whole(layers):
            total = layers[0]
            for layer in layers[1:]:
                total = total + layer
            return total

        parts = [
            (whole(mass), whole(third), whole(second)),
            (mass[0] + weighted(at_low, first), third[0], second[0]),
            (mass[n - 1] + weighted(at_high, first), third[n - 1], second[n - 1]),
        ]
        for part, (plain, lanewise, linewise) in enumerate(parts):
            flux_sum[part, x, 0] = copies_of * plain + third_weight * lanewise
            flux_sum[part, x, 1] = copies_of * linewise

    def divergence(x):
        rows = pl.ds(x * chunk, chunk)
        total = lane_operator(v_lane[1], v_vel[2, rows]) + row_operator(v_row[1], v_vel[1, rows])
        total = total + jnp.concatenate(
            odd_operator(transpose_list(derivative), layers_of(v_vel[0, rows])), axis=0
        )
        total = total + local[rows]
        crossed = jnp.where(
            is_upper, pltpu.roll(total, lanes - 1, axis=1), pltpu.roll(total, 1, axis=1)
        )
        local[rows] = total + shared * crossed

    def joined_sum(slot):
        plain = [column_sum[pl.ds(slot * 2 * slab + j, ey, stride=n)] for j in range(n)]
        linewise = [column_sum[pl.ds((slot * 2 + 1) * slab + j, ey, stride=n)] for j in range(n)]
        total = plain[0]
        for value in plain[1:]:
            total = total + value
        lower = plain[0] + weighted(at_low, linewise)
        upper = plain[n - 1] + weighted(at_high, linewise)
        below = jnp.where(first_line, 0.0, pltpu.roll(upper, 1, axis=0))
        above = jnp.where(last_line, 0.0, pltpu.roll(lower, ey - 1, axis=0))
        return total + below + above, lower, upper

    for x in range(ex):
        load_chunk(x)
        flux_chunk(x)

    def face_copies(phase):
        copies = []
        for index, (g, d) in enumerate(steps):
            if d == 0:
                source, target = side_send.at[phase, (g + 1) // 2], side_recv.at[phase, (1 - g) // 2]
            elif g == 0:
                source, target = row_send.at[phase, (d + 1) // 2], row_recv.at[phase, (1 - d) // 2]
            else:
                x = 0 if g < 0 else ex - 1
                source = row_send.at[phase, (d + 1) // 2, x]
                target = edge_recv.at[phase, (1 - g) // 2, (1 - d) // 2]
            copies.append(
                pltpu.make_async_remote_copy(
                    src_ref=source,
                    dst_ref=target,
                    send_sem=face_send.at[phase, index],
                    recv_sem=face_recv.at[phase, index],
                    device_id=neighbour(g, d),
                    device_id_type=MESH_IDS,
                )
            )
        return copies

    def pack_faces(field, phase):
        side_send[phase, 0] = field[pl.ds(0, slab)]
        side_send[phase, 1] = field[pl.ds(lay.rows - slab, slab)]
        for x in range(ex - 1):
            upper, lower = pl.ds((x + 1) * chunk - slab, slab), pl.ds((x + 1) * chunk, slab)
            both = field[upper] + field[lower]
            field[upper] = both
            field[lower] = both
        for x in range(ex):
            row_send[phase, 0, x] = field[pl.ds(x * chunk, n, stride=slab)]
            row_send[phase, 1, x] = field[pl.ds(x * chunk + slab - 1, n, stride=slab)]

    def send_faces(phase):
        copies = face_copies(phase)
        start_inside(copies, steps)
        return copies

    def join_faces(field, phase, copies):
        await_inside(copies, steps)
        whole_slab = jnp.zeros((slab, lanes), jnp.int32)
        head, tail = pl.ds(0, slab), pl.ds(lay.rows - slab, slab)
        field[head] = field[head] + jnp.where(whole_slab + group > 0, side_recv[phase, 0], 0.0)
        beyond = jnp.where(whole_slab + group < lay.groups - 1, side_recv[phase, 1], 0.0)
        field[tail] = field[tail] + beyond
        for d in range(2):
            low_edge = edge_recv[phase, 0, d, pl.ds(n - 1, n, stride=0)]
            high_edge = edge_recv[phase, 1, d, pl.ds(0, n, stride=0)]
            first = row_recv[phase, d, 0] + jnp.where(first_line & has_low_g, low_edge, 0.0)
            row_recv[phase, d, 0] = first
            last = row_recv[phase, d, ex - 1] + jnp.where(last_line & has_high_g, high_edge, 0.0)
            row_recv[phase, d, ex - 1] = last
            spot = 0 if d == 0 else n - 1
            for x in range(ex):
                outer = jnp.where((has_low_d, has_high_d)[d], row_recv[phase, d, x], 0.0)
                halo_lines[pl.ds(x * slab + spot, n, stride=n)] = outer
        starts = pl.ds(0, lines * ey, stride=n)
        ends = pl.ds(n - 1, lines * ey, stride=n)
        lower = field[starts].reshape(lines, ey, lanes)
        upper = field[ends].reshape(lines, ey, lanes)
        outside = halo_lines[...].reshape(lines, ey, lanes)
        from_below = jnp.where(first_line, outside, pltpu.roll(upper, 1, axis=1))
        from_above = jnp.where(last_line, outside, pltpu.roll(lower, ey - 1, axis=1))
        field[starts] = (lower + from_below).reshape(lines * ey, lanes)
        field[ends] = (upper + from_above).reshape(lines * ey, lanes)

    for part in range(2):
        column_sum[pl.ds(part * slab, slab)] = flux_sum[1, 0, part]
        column_sum[pl.ds((2 + part) * slab, slab)] = flux_sum[2, ex - 1, part]
        for x in range(ex):
            total = flux_sum[0, x, part]
            if x > 0:
                total = total + flux_sum[2, x - 1, part]
            if x < ex - 1:
                total = total + flux_sum[1, x + 1, part]
            column_sum[pl.ds((4 + 2 * x + part) * slab, slab)] = total
    for side in range(2):
        total, lower, upper = joined_sum(side)
        note_send[side] = total
        note_send[4 + 2 * side] = jnp.broadcast_to(lower[0:1], (ey, lanes))
        note_send[5 + 2 * side] = jnp.broadcast_to(upper[ey - 1 : ey], (ey, lanes))
    for x in range(ex):
        total, lower, upper = joined_sum(2 + x)
        sum_tile[x] = total
        note_send[2, pl.ds(x, 1)] = lower[0:1]
        note_send[3, pl.ds(x, 1)] = upper[ey - 1 : ey]

    def exists(g, d):
        found = (group + g >= 0) & (group + g < lay.groups)
        return found & (device + d >= 0) & (device + d < lay.devices)

    def start_inside(copies, ways):
        for copy, (g, d) in zip(copies, ways):
            pl.when(exists(g, d))(copy.start)

    def await_inside(copies, ways):
        for copy, (g, d) in zip(copies, ways):
            pl.when(exists(-g, -d))(copy.wait_recv)

    def await_sent(copies, ways):
        for copy, (g, d) in zip(copies, ways):
            pl.when(exists(g, d))(copy.wait_send)

    whole_line = jnp.zeros((n, lanes), jnp.int32)
    has_low_g, has_high_g = whole_line + group > 0, whole_line + group < lay.groups - 1
    has_low_d, has_high_d = whole_line + device > 0, whole_line + device < lay.devices - 1

    def note_slot(g, d):
        if d == 0:
            return (g + 1) // 2
        if g == 0:
            return 2 + (d + 1) // 2
        return 4 + 2 * ((g + 1) // 2) + (d + 1) // 2

    note_copies = [
        pltpu.make_async_remote_copy(
            src_ref=note_send.at[note_slot(g, d)],
            dst_ref=note_recv.at[note_slot(-g, -d)],
            send_sem=note_sent.at[index],
            recv_sem=note_got.at[index],
            device_id=neighbour(g, d),
            device_id_type=MESH_IDS,
        )
        for index, (g, d) in enumerate(steps)
    ]

    pl.semaphore_wait(barrier, len(steps) + lay.pack - 1 + lay.far - 1)
    start_inside(note_copies, steps)
    late_loads[0].wait()
    for x in range(ex):
        layers = layers_of(v_rs[pl.ds(x * chunk, chunk)])
        total = layers[0]
        for layer in layers[1:]:
            total = total + layer
        column_sum[pl.ds(x * slab, slab)] = total
    for x in range(ex):
        total = column_sum[pl.ds(x * slab, ey, stride=n)]
        for j in range(1, n):
            total = total + column_sum[pl.ds(x * slab + j, ey, stride=n)]
        sum_tile[x] = total - sum_tile[x]
    late_loads[1].wait()
    def rim_block(line, carry):
        spot = pl.ds(pl.multiple_of(line * lanes, lanes), lanes)
        for x in range(ex):
            rim_send[0, line, pl.ds(x, 1)] = v_fac[pl.ds(x * ey, 1), spot]
            rim_send[1, line, pl.ds(x, 1)] = v_fac[pl.ds(x * ey + ey - 1, 1), spot]
        return carry

    lax.fori_loop(0, lay.coarse_lines, rim_block, 0)

    rim_copies = [
        pltpu.make_async_remote_copy(
            src_ref=rim_send.at[(d + 1) // 2],
            dst_ref=rim_recv.at[(1 - d) // 2],
            send_sem=rim_sem.at[0, (d + 1) // 2],
            recv_sem=rim_sem.at[1, (d + 1) // 2],
            device_id=neighbour(0, d),
            device_id_type=MESH_IDS,
        )
        for d in (-1, 1)
    ]
    rim_ways = [(0, -1), (0, 1)]
    start_inside(rim_copies, rim_ways)
    for x in range(ex):
        divergence(x)
    pack_faces(local, 0)
    first_copies = send_faces(0)
    await_inside(note_copies, steps)
    sums = []
    for x in range(ex):
        total = sum_tile[x]
        ends = []
        for d in range(2):
            end = note_recv[2 + d, pl.ds(x, ey, stride=0)]
            if x == 0:
                end = end + jnp.where(has_low_g, note_recv[4 + d], 0.0)
            if x == ex - 1:
                end = end + jnp.where(has_high_g, note_recv[6 + d], 0.0)
            ends.append(jnp.where((has_low_d, has_high_d)[d], end, 0.0))
        if x == 0:
            total = total - jnp.where(has_low_g, note_recv[0], 0.0)
        if x == ex - 1:
            total = total - jnp.where(has_high_g, note_recv[1], 0.0)
        total = total - jnp.where(first_line, ends[0], 0.0) - jnp.where(last_line, ends[1], 0.0)
        sums.append(total)
    means = jnp.sum(jnp.concatenate(sums, axis=0), axis=1, keepdims=True)
    means = jnp.broadcast_to(means * (1.0 / float(n * n * lanes)), (columns, lanes))

    def inner_block(block, carry):
        for k in range(8):
            line = block * 8 + k
            piece = v_fac[:, pl.ds(pl.multiple_of(line * lanes, lanes), lanes)] * means
            total = piece[0:8]
            for start in range(8, columns, 8):
                total = total + piece[start : start + 8]
            inner_part[pl.ds(pl.multiple_of(line * 8, 8), 8)] = total
        return carry

    lax.fori_loop(0, lay.coarse_lines // 8, inner_block, 0)
    for index in range(lay.pack):
        base = index * lay.share * 8
        total = inner_part[pl.ds(base, lay.share, stride=8)]
        for k in range(1, 8):
            total = total + inner_part[pl.ds(base + k, lay.share, stride=8)]
        near_src[index] = total

    def exchange(stage, count, own, device_of, source_of, buffer):
        def send(offset, carry):
            index = lax.rem(own + offset, count)
            pltpu.make_async_remote_copy(
                src_ref=source_of(index),
                dst_ref=buffer.at[own],
                send_sem=sum_send.at[stage],
                recv_sem=sum_recv.at[stage],
                device_id=device_of(index),
                device_id_type=MESH_IDS,
            ).start()
            return carry

        for offset in sorted(range(1, count), key=far_hops if stage == 1 else near_hops, reverse=True):
            send(offset, 0)

    def await_exchange(stage, count, buffer, sem):
        part = buffer.at[pl.ds(0, count - 1)]
        pltpu.make_async_copy(part, part, sem.at[stage]).wait()

    exchange(0, lay.pack, near_id, near_device, lambda index: near_src.at[index], near_in)
    near_in[near_id] = near_src[near_id]


    await_exchange(0, lay.pack, near_in, sum_recv)
    far_in[far_id] = jnp.sum(near_in[...], axis=0)
    exchange(1, lay.far, far_id, far_device, lambda index: far_in.at[far_id], far_in)

    join_faces(local, 0, first_copies)
    for x in range(ex):
        rows = pl.ds(x * chunk, chunk)
        residual[rows] = v_rs[rows] - local[rows]

    for copy in late_loads[2:]:
        copy.wait()

    def solve_chunk(x):
        rows = pl.ds(x * chunk, chunk)
        field = jnp.concatenate(to_modes(vectors, layers_of(residual[rows])), axis=0)
        field = row_operator(v_row[2], field)
        field = lane_operator(v_lane[2], field) * v_fdm[rows]
        field = lane_operator(v_lane[3], field)
        field = row_operator(v_row[3], field)
        correction[rows] = jnp.concatenate(from_modes(vectors, layers_of(field)), axis=0)

    for x in range(ex):
        solve_chunk(x)
    pack_faces(correction, 1)
    second_copies = send_faces(1)

    await_exchange(1, lay.far, far_in, sum_recv)
    full_in[near_id] = jnp.sum(far_in[...], axis=0)
    exchange(2, lay.pack, near_id, near_device, lambda index: full_in.at[near_id], full_in)

    await_inside(rim_copies, rim_ways)

    await_exchange(2, lay.pack, full_in, sum_recv)

    def value_block(index, totals):
        inside, left, right = totals
        for k in range(lay.share):
            line = index * lay.share + k
            value = jnp.broadcast_to(full_in[index, pl.ds(k, 1)], (columns, lanes))
            spot = pl.ds(pl.multiple_of(line * lanes, lanes), lanes)
            inside = inside + v_fac[:, spot] * value
            left = left + rim_recv[0, line] * value[:ex]
            right = right + rim_recv[1, line] * value[:ex]
        return inside, left, right

    none = jnp.zeros((ex, lanes), jnp.float32)
    inside, left, right = lax.fori_loop(
        0, lay.pack, value_block, (jnp.zeros((columns, lanes), jnp.float32), none, none)
    )
    inside = jnp.broadcast_to(jnp.sum(inside, axis=1, keepdims=True), (columns, lanes))
    rim_line = jnp.zeros((ex, 1), jnp.int32) + device
    left = jnp.where(rim_line > 0, jnp.sum(left, axis=1, keepdims=True), 0.0)
    right = jnp.where(rim_line < lay.devices - 1, jnp.sum(right, axis=1, keepdims=True), 0.0)
    for x in range(ex):
        grid[0, 1 + x] = inside[x * ey : (x + 1) * ey]
        grid[1, 1 + x] = jnp.broadcast_to(left[x : x + 1], (ey, lanes))
        grid[2, 1 + x] = jnp.broadcast_to(right[x : x + 1], (ey, lanes))
    for part in range(3):
        ring_out[0, part] = grid[part, 1]
        ring_out[1, part] = grid[part, ex]
    ring_copies = [
        pltpu.make_async_remote_copy(
            src_ref=ring_out.at[(g + 1) // 2],
            dst_ref=ring_in.at[(1 - g) // 2],
            send_sem=ring_sem.at[0, (g + 1) // 2],
            recv_sem=ring_sem.at[1, (g + 1) // 2],
            device_id=neighbour(g, 0),
            device_id_type=MESH_IDS,
        )
        for g in (-1, 1)
    ]
    ring_ways = [(-1, 0), (1, 0)]
    start_inside(ring_copies, ring_ways)
    join_faces(correction, 1, second_copies)
    await_inside(ring_copies, ring_ways)
    for part in range(3):
        grid[part, 0] = jnp.where(has_low_g, ring_in[0, part], 0.0)
        grid[part, ex + 1] = jnp.where(has_high_g, ring_in[1, part], 0.0)

    await_sent(note_copies, steps)
    await_sent(ring_copies, ring_ways)
    await_sent(first_copies, steps)
    await_sent(rim_copies, rim_ways)
    await_sent(second_copies, steps)
    await_exchange(0, lay.pack, near_in, sum_send)
    await_exchange(1, lay.far, far_in, sum_send)
    await_exchange(2, lay.pack, full_in, sum_send)


def finish_kernel(lay, residual, solved, grid, out_residual, out_correction, staged, tile, sem):
    ex, n, ey, lanes, slab, chunk = lay.ex, lay.n, lay.ey, lay.lanes, lay.slab, lay.chunk
    copies = [pltpu.make_async_copy(residual, out_residual, sem.at[0])]
    copies[0].start()
    lane_index = lax.broadcasted_iota(jnp.int32, (1, lanes), 1)
    lane_node = lax.rem(lane_index, n)
    shared = ((lane_node == n - 1) & (lane_index != lanes - 1)) | (
        (lane_node == 0) & (lane_index != 0)
    )
    copies_of = jnp.where(shared, 2.0, 1.0).astype(jnp.float32)
    line_index = lax.broadcasted_iota(jnp.int32, (ey, lanes), 0)
    first_line, last_line = line_index == 0, line_index == ey - 1
    for x in range(ex):
        for part in range(3):
            sides = []
            for side in range(3):
                value = grid[side, x + 1]
                if part == 0:
                    value = value + grid[side, x]
                elif part == 2:
                    value = value + grid[side, x + 2]
                sides.append(value * copies_of)
            inside, left, right = sides
            below = jnp.where(first_line, left, pltpu.roll(inside, 1, axis=0))
            above = jnp.where(last_line, right, pltpu.roll(inside, ey - 1, axis=0))
            for j in range(n):
                value = inside
                if j == 0:
                    value = inside + below
                elif j == n - 1:
                    value = inside + above
                tile[x, part, pl.ds(j, ey, stride=n)] = value
        for layer in range(n):
            part = 0 if layer == 0 else 2 if layer == n - 1 else 1
            spot = pl.ds(x * chunk + layer * slab, slab)
            staged[spot] = solved[spot] + tile[x, part]
        rows = pl.ds(x * chunk, chunk)
        copy = pltpu.make_async_copy(staged.at[rows], out_correction.at[rows], sem.at[1 + x])
        copy.start()
        copies.append(copy)
    for copy in copies:
        copy.wait()


def solution(mesh):
    groups, devices = mesh.shape["grp"], mesh.shape["dev"]

    def body(adjoint, right_side, velocity, conductivity, mass_term, fdm_inverse, coarse_factor):
        ex, n, ey, _, lanes = adjoint.shape
        lay = Layout(ex, n, ey, lanes, groups, devices, coarse_factor.shape[1])
        derivative, vectors, lane_tables, row_tables = operator_tables(n, lanes)
        flat = (lay.rows, lanes)
        f32, bf16 = jnp.float32, jnp.bfloat16
        hbm = pl.BlockSpec(memory_space=pltpu.HBM)
        vmem = pl.BlockSpec(memory_space=pltpu.VMEM)
        scratch = [
            pltpu.VMEM(flat, f32),
            pltpu.VMEM(flat, f32),
            pltpu.VMEM((3,) + flat, f32),
            pltpu.VMEM(flat, f32),
            pltpu.VMEM(flat, f32),
            pltpu.VMEM(flat, f32),
            pltpu.VMEM(coarse_factor.shape, f32),
            pltpu.VMEM(lane_tables.shape, bf16),
            pltpu.VMEM(row_tables.shape, bf16),
            pltpu.VMEM((3, ex, 2, lay.slab, lanes), f32),
            pltpu.VMEM(flat, f32),
            pltpu.VMEM((2, 2, lay.slab, lanes), f32),
            pltpu.VMEM((2, 2, lay.slab, lanes), f32),
            pltpu.VMEM((2, 2, ex, n, lanes), f32),
            pltpu.VMEM((2, 2, ex, n, lanes), f32),
            pltpu.VMEM((2, 2, 2, n, lanes), f32),
            pltpu.VMEM((lay.lines * ey, lanes), f32),
            pltpu.VMEM((2 * (2 + ex) * lay.slab, lanes), f32),
            pltpu.VMEM((lay.coarse_lines * 8, lanes), f32),
            pltpu.VMEM((lay.pack, lay.share, lanes), f32),
            pltpu.VMEM((lay.pack, lay.share, lanes), f32),
            pltpu.VMEM((lay.far, lay.share, lanes), f32),
            pltpu.VMEM((lay.pack, lay.share, lanes), f32),
            pltpu.VMEM((ex, ey, lanes), f32),
            pltpu.VMEM((8, ey, lanes), f32),
            pltpu.VMEM((8, ey, lanes), f32),
            pltpu.VMEM((2, lay.coarse_lines, ex, lanes), f32),
            pltpu.VMEM((2, lay.coarse_lines, ex, lanes), f32),
            pltpu.VMEM((2, 3, ey, lanes), f32),
            pltpu.VMEM((2, 3, ey, lanes), f32),
            pltpu.SemaphoreType.DMA((6, 4)),
            pltpu.SemaphoreType.DMA((2, 8)),
            pltpu.SemaphoreType.DMA((2, 8)),
            pltpu.SemaphoreType.DMA((8,)),
            pltpu.SemaphoreType.DMA((8,)),
            pltpu.SemaphoreType.DMA((2, 2)),
            pltpu.SemaphoreType.DMA((2, 2)),
            pltpu.SemaphoreType.DMA((3,)),
            pltpu.SemaphoreType.DMA((3,)),
        ]
        grid = (3, ex + 2, ey, lanes)
        residual, solved, grid_values = pl.pallas_call(
            functools.partial(step_kernel, lay, derivative, vectors),
            out_shape=[
                jax.ShapeDtypeStruct(flat, f32),
                jax.ShapeDtypeStruct(flat, f32),
                jax.ShapeDtypeStruct(grid, f32),
            ],
            in_specs=[hbm] * 9,
            out_specs=[vmem] * 3,
            scratch_shapes=scratch,
            compiler_params=pltpu.CompilerParams(
                collective_id=0, has_side_effects=True, vmem_limit_bytes=40 * 1024 * 1024
            ),
            name="adjoint_step",
        )(
            *[
                pltpu.with_memory_space_constraint(array, pltpu.HBM)
                for array in (
                    adjoint.reshape(flat),
                    right_side.reshape(flat),
                    velocity.reshape((3,) + flat),
                    conductivity.reshape(flat),
                    mass_term.reshape(flat),
                    fdm_inverse.reshape(flat),
                    coarse_factor,
                    jnp.asarray(lane_tables),
                    jnp.asarray(row_tables),
                )
            ]
        )
        residual, correction = pl.pallas_call(
            functools.partial(finish_kernel, lay),
            out_shape=[pltpu.HBM(flat, f32)] * 2,
            in_specs=[vmem] * 3,
            out_specs=[hbm] * 2,
            scratch_shapes=[
                pltpu.VMEM(flat, f32),
                pltpu.VMEM((ex, 3, lay.slab, lanes), f32),
                pltpu.SemaphoreType.DMA((1 + ex,)),
            ],
            name="finish",
        )(
            *[
                pltpu.with_memory_space_constraint(array, pltpu.VMEM)
                for array in (residual, solved, grid_values)
            ]
        )
        return residual.reshape(adjoint.shape), correction.reshape(adjoint.shape)

    field = P("grp", None, "dev", None, None)
    in_specs = (
        field,
        field,
        P(None, "grp", None, "dev", None, None),
        field,
        field,
        field,
        P(("grp", "dev"), None),
    )
    return jax.shard_map(
        body, mesh=mesh, in_specs=in_specs, out_specs=(field, field), check_vma=False
    )
```
